256 devices in a mesh: gx: 8 (over z_lo, x), gy: 32 (over z_hi, y, core).
Axes of the slice: x: 4, y: 4, z: 8 (z_hi: 4, z_lo: 2; z = z_hi * 2 + z_lo), core: 2. Of those that a mesh axis runs over, the one named last changes fastest.
Arguments:
- snapshot: float32 [384, 384, 32, 16], P('gx', 'gy'), may hold values from -6 to 6
- start_x: float32 [384, 96], replicated, may hold values from -0.3125 to 0.3125
- start_y: float32 [384, 96], replicated, may hold values from -0.3125 to 0.3125
Outputs:
- basis_x: float32 [384, 96], P('gx')
- basis_y: float32 [384, 96], P('gy')
- core: float32 [96, 96, 32, 16], P('gx', 'gy')
The draws below stay inside these ranges and needn't reach their ends.
All inputs are finite; a program needn't handle non-finite values.
Results may differ from the reference program's by a relative error of at most 0.0003.
Values sent between devices are 32-bit elements; how exact they have to be, the bound alone decides.
A program may use at most 64 MiB of HBM per device.

```python
import math
import jax
import jax.numpy as jnp
from jax import lax

NX = 384
NY = 384
NZ = 32
V = 16
R = 96
ITERS = 4


def build_field(factor_x, factor_y, inner, noise, amplitude):
    ratio = 20.0
    total = sum((ratio ** (-k / (R - 1)) for k in range(R)))
    weight_struct = 1.0 / total
    sigma_noise = math.sqrt(NX / (40.0 * total))
    levels = jnp.arange(R, dtype=jnp.float32) / float(R - 1)
    decay = jnp.power(jnp.float32(ratio), -0.5 * levels)
    scaled = inner * (weight_struct * decay[:, None, None] * decay[None, :, None])
    middle = jnp.einsum('yj,kjc->kyc', factor_y, scaled, precision=lax.Precision.HIGHEST)
    field = jnp.einsum('xk,kyc->xyc', factor_x, middle, precision=lax.Precision.HIGHEST)
    field = amplitude * (field + sigma_noise * noise)
    field = jnp.clip(field, -6.0, 6.0)
    return field.reshape(NX, NY, NZ, V).astype(jnp.float32)


def draw_snapshot(key, part):
    key = jax.random.fold_in(key, 7)
    key_x, key_y, key_inner, key_noise = jax.random.split(key, 4)
    columns = NZ * V
    factor_x = jax.random.normal(key_x, (NX, R), jnp.float32)
    factor_y = jax.random.normal(key_y, (NY, R), jnp.float32)
    inner = jax.random.normal(key_inner, (R, R, columns), jnp.float32)
    noise = jax.random.normal(key_noise, (NX, NY, columns), jnp.float32)
    amplitude = 1.0
    return build_field(factor_x, factor_y, inner, noise, amplitude)


def scatter_about(own_key, shape, width, most, kind=jnp.bfloat16):
    entries = jax.random.normal(own_key, shape, jnp.float32) * width
    return jnp.minimum(jnp.maximum(entries, -most), most).astype(kind)


def setup_inputs(seed: int = 0) -> dict:
    keys = jax.random.split(jax.random.key(seed), 4)
    snapshot = draw_snapshot(jax.random.fold_in(keys[3], 71), 0)
    start_x = scatter_about(keys[1], (NX, R), NX ** -0.5, 0.3125, jnp.float32)
    start_y = scatter_about(keys[2], (NY, R), NY ** -0.5, 0.3125, jnp.float32)
    return {"snapshot": snapshot, "start_x": start_x, "start_y": start_y}


HIGH = lax.Precision.HIGHEST

def orthonormalize(matrix):
    cross = jnp.dot(matrix.T, matrix, precision=HIGH)
    lower = jnp.linalg.cholesky(cross)
    return lax.linalg.triangular_solve(lower, matrix, left_side=False, lower=True, transpose_a=True)

def iterate(gram, start):
    basis = start
    for step in range(ITERS):
        basis = orthonormalize(jnp.dot(gram, basis, precision=HIGH))
    return basis

def reference(snapshot, start_x, start_y):
    flat = snapshot.reshape(NX, NY * NZ * V)
    gram_x = jnp.dot(flat, flat.T, precision=HIGH)
    basis_x = iterate(gram_x, start_x)
    reduced = jnp.dot(basis_x.T, flat, precision=HIGH).reshape(R, NY, NZ * V)
    gram_y = jnp.einsum('ryc,rwc->yw', reduced, reduced, precision=HIGH)
    basis_y = iterate(gram_y, start_y)
    core = jnp.einsum('ys,ryc->rsc', basis_y, reduced, precision=HIGH).reshape(R, R, NZ, V)
    return (basis_x, basis_y, core)
```

```python
import functools

import jax
import jax.numpy as jnp
from jax import lax
from jax.experimental import pallas as pl
from jax.experimental.pallas import tpu as pltpu
from jax.sharding import PartitionSpec as P

ITERS = 4
HIGH = lax.Precision.HIGHEST
MESH = pl.DeviceIdType.MESH
F32 = jnp.float32

NXC, NYC, NZC = 4, 4, 8
GX, GY = 8, 32
PLANE = NXC * NYC


def position():
    gx, gy = lax.axis_index("gx"), lax.axis_index("gy")
    z = (gy // 8) * 2 + gx // 4
    plane = ((gy // 2) % 4) * 4 + gx % 4
    return gx, gy, z, plane, gy % 2


def device(z, plane, core):
    return ((z % 2) * 4 + plane % 4, (z // 2) * 8 + (plane // 4) * 2 + core)


def loop(low, high, body):
    def step(i, carry):
        body(i)
        return carry

    lax.fori_loop(low, high, step, 0)


def signal(sem, where):
    pl.semaphore_signal(sem, inc=1, device_id=where, device_id_type=MESH)


def greet_sum(barrier):
    _, _, z, plane, core = position()
    signal(barrier, device(z, plane, 1 - core))
    loop(1, PLANE, lambda d: signal(barrier, device(z, (plane + d) % PLANE, core)))
    loop(1, NZC, lambda d: signal(barrier, device((z + d) % NZC, plane, core)))
    return 1 + (PLANE - 1) + (NZC - 1)


def sum_scratch():
    return [
        pltpu.VMEM((2, PLANE, 24, 128), F32),
        pltpu.VMEM((PLANE, 24, 128), F32),
        pltpu.VMEM((PLANE, 24, 128), F32),
        pltpu.VMEM((NZC, 24, 128), F32),
        pltpu.SemaphoreType.DMA((2, 2)),
        pltpu.SemaphoreType.DMA((2, 2, PLANE)),
        pltpu.SemaphoreType.DMA((2, NZC)),
    ]


def all_sum(part, out, half, slots, zslots, core_sem, plane_sem, z_sem):
    _, _, z, plane, core = position()

    def core_copy(src, dst, k):
        return pltpu.make_async_remote_copy(
            src_ref=src, dst_ref=dst, send_sem=core_sem.at[k, 0], recv_sem=core_sem.at[k, 1],
            device_id=device(z, plane, 1 - core), device_id_type=MESH)

    copy = core_copy(part.at[1 - core], half, 0)
    copy.start()
    copy.wait()
    half[...] += part[core]

    def scatter(d):
        to = (plane + d) % PLANE
        return pltpu.make_async_remote_copy(
            src_ref=half.at[to], dst_ref=slots.at[d],
            send_sem=plane_sem.at[0, 0, d], recv_sem=plane_sem.at[0, 1, d],
            device_id=device(z, to, core), device_id_type=MESH)

    loop(1, PLANE, lambda d: scatter(d).start())
    loop(1, PLANE, lambda d: scatter(d).wait())
    total = half[plane]
    for d in range(1, PLANE):
        total += slots[d]
    zslots[z] = total

    def spread(d):
        return pltpu.make_async_remote_copy(
            src_ref=zslots.at[z], dst_ref=zslots.at[z],
            send_sem=z_sem.at[0, d], recv_sem=z_sem.at[1, d],
            device_id=device((z + d) % NZC, plane, core), device_id_type=MESH)

    loop(1, NZC, lambda d: spread(d).start())
    loop(1, NZC, lambda d: spread(d).wait())
    total = zslots[0]
    for k in range(1, NZC):
        total += zslots[k]
    out[core, plane] = total

    def gather(d):
        return pltpu.make_async_remote_copy(
            src_ref=out.at[core, plane], dst_ref=out.at[core, plane],
            send_sem=plane_sem.at[1, 0, d], recv_sem=plane_sem.at[1, 1, d],
            device_id=device(z, (plane + d) % PLANE, core), device_id_type=MESH)

    loop(1, PLANE, lambda d: gather(d).start())
    loop(1, PLANE, lambda d: gather(d).wait())
    copy = core_copy(out.at[core], out.at[core], 1)
    copy.start()
    copy.wait()


PAIRS = [(0, 0), (0, 1), (0, 2), (1, 1), (1, 2), (2, 2)]


def gram_blocks(rows, part):
    for k, (a, b) in enumerate(PAIRS):
        block = lax.dot_general(
            rows[128 * a:128 * a + 128, :], rows[128 * b:128 * b + 128, :],
            (((1,), (1,)), ((), ())), precision=HIGH, preferred_element_type=F32)
        flat = k * 128
        while flat < k * 128 + 128:
            inside = flat % 24
            size = min(24 - inside, k * 128 + 128 - flat)
            slab = flat // 24
            part[slab // PLANE, slab % PLANE, inside:inside + size, :] = block[flat - k * 128:flat - k * 128 + size]
            flat += size


def unpack_gram(packed):
    blocks = packed.reshape(6, 128, 128)
    u = {pair: blocks[k] for k, pair in enumerate(PAIRS)}
    return jnp.block([[u[(a, b)] if a <= b else u[(b, a)].T for b in range(3)] for a in range(3)])


def field_kernel(cells, field, gram, send, send_sem, recv_sem, *sums):
    gx, gy, _, _, _ = position()
    barrier = pltpu.get_barrier_semaphore()
    loop(1, GX, lambda d: signal(barrier, ((gx + d) % GX, gy)))
    count = greet_sum(barrier)
    pl.semaphore_wait(barrier, GX - 1 + count)

    def turn(to):
        for k in range(6):
            start = pl.multiple_of(to * 64, 64)
            pair = [cells[2 * k + h, pl.ds(start, 64), :] for h in range(2)]
            yield slice(128 * k, 128 * k + 128), jnp.concatenate(pair, axis=0).T

    def copy(d):
        to = (gx + d) % GX
        return pltpu.make_async_remote_copy(
            src_ref=send.at[to], dst_ref=field.at[gx],
            send_sem=send_sem.at[d], recv_sem=recv_sem.at[d],
            device_id=(to, gy), device_id_type=MESH)

    def push(d):
        to = (gx + d) % GX
        for lanes, block in turn(to):
            send[to, :, lanes] = block
        copy(d).start()

    loop(1, GX, push)
    for lanes, block in turn(gx):
        field[gx, :, lanes] = block
    loop(1, GX, lambda d: copy(d).wait())
    gram_blocks(field[...].reshape(384, 768), sums[0])
    all_sum(sums[0], gram, *sums[1:])


def planes_kernel(reduced, rows, gram, send, planes, send_sem, recv_sem, *sums):
    gx, gy, _, _, _ = position()
    barrier = pltpu.get_barrier_semaphore()
    loop(1, GY, lambda d: signal(barrier, (gx, (gy + d) % GY)))
    count = greet_sum(barrier)
    pl.semaphore_wait(barrier, GY - 1 + count)

    for k in range(GY):
        send[k] = reduced[3 * k:3 * k + 3, :]

    def copy(d):
        to = (gy + d) % GY
        return pltpu.make_async_remote_copy(
            src_ref=send.at[to], dst_ref=planes.at[gy],
            send_sem=send_sem.at[d], recv_sem=recv_sem.at[d],
            device_id=(gx, to), device_id_type=MESH)

    loop(1, GY, lambda d: copy(d).start())
    planes[gy] = send[gy]
    loop(1, GY, lambda d: copy(d).wait())
    for y in range(12):
        parts = [planes[:, r, 64 * y:64 * y + 64] for r in range(3)]
        parts.append(jnp.zeros((GY, 64), F32))
        for k in range(2):
            rows[k, pl.ds(y, GY, stride=12), :] = jnp.concatenate(parts[2 * k:2 * k + 2], axis=1)
    gram_blocks(jnp.concatenate([rows[0], rows[1]], axis=1), sums[0])
    all_sum(sums[0], gram, *sums[1:])


def core_kernel(part, out, send, send_sem, recv_sem):
    gx, gy, _, _, _ = position()
    home = gy // 4
    slot = gx * 4 + gy % 4
    barrier = pltpu.get_barrier_semaphore()
    loop(0, GY, lambda k: signal(barrier, (k // 4, gx * 4 + k % 4)))
    pl.semaphore_wait(barrier, GY)

    for k in range(GY):
        send[k] = part[3 * k:3 * k + 3, :]

    def copy(k):
        return pltpu.make_async_remote_copy(
            src_ref=send.at[k], dst_ref=out.at[slot],
            send_sem=send_sem.at[k], recv_sem=recv_sem.at[slot],
            device_id=(home, k), device_id_type=MESH)

    def arrival(k):
        return pltpu.make_async_remote_copy(
            src_ref=send.at[k], dst_ref=out.at[k],
            send_sem=send_sem.at[k], recv_sem=recv_sem.at[k],
            device_id=(home, k), device_id_type=MESH)

    def go(k):
        mine = (home == gx) & (k == gy)

        @pl.when(jnp.logical_not(mine))
        def _():
            copy(k).start()

        @pl.when(mine)
        def _():
            out[slot] = send[k]

    def finish(k):
        @pl.when(jnp.logical_not((home == gx) & (k == gy)))
        def _():
            copy(k).wait_send()

        @pl.when(jnp.logical_not((home == gx) & (k == slot)))
        def _():
            arrival(k).wait_recv()

    loop(0, GY, go)
    loop(0, GY, finish)


def params(number):
    return pltpu.CompilerParams(
        collective_id=number, has_side_effects=True, vmem_limit_bytes=40 * 1024 * 1024)


VM = pl.BlockSpec(memory_space=pltpu.VMEM)


def iterate(gram, start):
    own = start
    for _ in range(ITERS):
        image = jnp.dot(own, gram, precision=HIGH)
        cross = jnp.dot(image, image.T, precision=HIGH)
        lower = jnp.linalg.cholesky(cross)
        own = lax.linalg.triangular_solve(lower, image, left_side=True, lower=True)
    return own


def local(snapshot, start_x, start_y):
    gx, gy = lax.axis_index("gx"), lax.axis_index("gy")
    cells = jnp.transpose(snapshot, (1, 2, 3, 0)).reshape(12, 512, 48)
    field, gram_x = pl.pallas_call(
        field_kernel,
        out_shape=[
            jax.ShapeDtypeStruct((GX, 48, 768), F32),
            jax.ShapeDtypeStruct((2, PLANE, 24, 128), F32),
        ],
        in_specs=[VM],
        out_specs=[VM, VM],
        scratch_shapes=[
            pltpu.VMEM((GX, 48, 768), F32),
            pltpu.SemaphoreType.DMA((GX,)),
            pltpu.SemaphoreType.DMA((GX,)),
        ] + sum_scratch(),
        compiler_params=params(1),
        name="field",
    )(cells)
    basis_x = iterate(unpack_gram(gram_x), start_x.T)
    reduced = jnp.dot(basis_x, field.reshape(384, 768), precision=HIGH)
    rows, gram_y = pl.pallas_call(
        planes_kernel,
        out_shape=[
            jax.ShapeDtypeStruct((2, 384, 128), F32),
            jax.ShapeDtypeStruct((2, PLANE, 24, 128), F32),
        ],
        in_specs=[VM],
        out_specs=[VM, VM],
        scratch_shapes=[
            pltpu.VMEM((GY, 3, 768), F32),
            pltpu.VMEM((GY, 3, 768), F32),
            pltpu.SemaphoreType.DMA((GY,)),
            pltpu.SemaphoreType.DMA((GY,)),
        ] + sum_scratch(),
        compiler_params=params(2),
        name="planes",
    )(reduced)
    basis_y = iterate(unpack_gram(gram_y), start_y.T)
    core = jnp.dot(basis_y, jnp.concatenate([rows[0], rows[1, :, :64]], axis=1), precision=HIGH)
    pieces = pl.pallas_call(
        core_kernel,
        out_shape=jax.ShapeDtypeStruct((GY, 3, 192), F32),
        in_specs=[VM],
        out_specs=VM,
        scratch_shapes=[
            pltpu.VMEM((GY, 3, 192), F32),
            pltpu.SemaphoreType.DMA((GY,)),
            pltpu.SemaphoreType.DMA((GY,)),
        ],
        compiler_params=params(3),
        name="core",
    )(core)
    pieces = pieces.reshape(8, 4, 3, 3, 4, 16)
    core = jnp.transpose(pieces, (1, 3, 2, 0, 4, 5)).reshape(12, 3, 32, 16)
    own_x = lax.dynamic_slice(basis_x, (0, gx * 48), (96, 48)).T
    own_y = lax.dynamic_slice(basis_y, (0, gy * 12), (96, 12)).T
    return (own_x, own_y, core)


def solution(mesh):
    in_specs = (P("gx", "gy", None, None), P(), P())
    out_specs = (P("gx", None), P("gy", None), P("gx", "gy", None, None))
    return jax.shard_map(local, mesh=mesh, in_specs=in_specs, out_specs=out_specs, check_vma=False)
```

```python
import functools

import jax
import jax.numpy as jnp
from jax import lax
from jax.experimental import pallas as pl
from jax.experimental.pallas import tpu as pltpu
from jax.sharding import PartitionSpec as P

ITERS = 4
HIGH = lax.Precision.HIGHEST
MESH = pl.DeviceIdType.MESH
F32 = jnp.float32
BF16 = jnp.bfloat16

NXC, NYC, NZC = 4, 4, 8
GX, GY = 8, 32
PLANE = NXC * NYC


def position():
    gx, gy = lax.axis_index("gx"), lax.axis_index("gy")
    z = (gy // 8) * 2 + gx // 4
    plane = ((gy // 2) % 4) * 4 + gx % 4
    return gx, gy, z, plane, gy % 2


def device(z, plane, core):
    return ((z % 2) * 4 + plane % 4, (z // 2) * 8 + (plane // 4) * 2 + core)


def loop(low, high, body):
    def step(i, carry):
        body(i)
        return carry

    lax.fori_loop(low, high, step, 0)


def signal(sem, where):
    pl.semaphore_signal(sem, inc=1, device_id=where, device_id_type=MESH)


def greet_sum(barrier):
    _, _, z, plane, core = position()
    signal(barrier, device(z, plane, 1 - core))
    loop(1, PLANE, lambda d: signal(barrier, device(z, (plane + d) % PLANE, core)))
    loop(1, NZC, lambda d: signal(barrier, device((z + d) % NZC, plane, core)))
    return 1 + (PLANE - 1) + (NZC - 1)


def sum_scratch():
    return [
        pltpu.VMEM((2, PLANE, 24, 128), F32),
        pltpu.VMEM((PLANE, 24, 128), F32),
        pltpu.VMEM((PLANE, 24, 128), F32),
        pltpu.VMEM((NZC, 24, 128), F32),
        pltpu.SemaphoreType.DMA((2, 2)),
        pltpu.SemaphoreType.DMA((2, 2, PLANE)),
        pltpu.SemaphoreType.DMA((2, NZC)),
    ]


def all_sum(part, out, half, slots, zslots, core_sem, plane_sem, z_sem):
    _, _, z, plane, core = position()

    def core_copy(src, dst, k):
        return pltpu.make_async_remote_copy(
            src_ref=src, dst_ref=dst, send_sem=core_sem.at[k, 0], recv_sem=core_sem.at[k, 1],
            device_id=device(z, plane, 1 - core), device_id_type=MESH)

    copy = core_copy(part.at[1 - core], half, 0)
    copy.start()
    copy.wait()
    half[...] += part[core]

    def scatter(d):
        to = (plane + d) % PLANE
        return pltpu.make_async_remote_copy(
            src_ref=half.at[to], dst_ref=slots.at[d],
            send_sem=plane_sem.at[0, 0, d], recv_sem=plane_sem.at[0, 1, d],
            device_id=device(z, to, core), device_id_type=MESH)

    loop(1, PLANE, lambda d: scatter(d).start())
    loop(1, PLANE, lambda d: scatter(d).wait())
    total = half[plane]
    for d in range(1, PLANE):
        total += slots[d]
    zslots[z] = total

    def spread(d):
        return pltpu.make_async_remote_copy(
            src_ref=zslots.at[z], dst_ref=zslots.at[z],
            send_sem=z_sem.at[0, d], recv_sem=z_sem.at[1, d],
            device_id=device((z + d) % NZC, plane, core), device_id_type=MESH)

    loop(1, NZC, lambda d: spread(d).start())
    loop(1, NZC, lambda d: spread(d).wait())
    total = zslots[0]
    for k in range(1, NZC):
        total += zslots[k]
    out[core, plane] = total

    def gather(d):
        return pltpu.make_async_remote_copy(
            src_ref=out.at[core, plane], dst_ref=out.at[core, plane],
            send_sem=plane_sem.at[1, 0, d], recv_sem=plane_sem.at[1, 1, d],
            device_id=device(z, (plane + d) % PLANE, core), device_id_type=MESH)

    loop(1, PLANE, lambda d: gather(d).start())
    loop(1, PLANE, lambda d: gather(d).wait())
    copy = core_copy(out.at[core], out.at[core], 1)
    copy.start()
    copy.wait()


PAIRS = [(0, 0), (0, 1), (0, 2), (1, 1), (1, 2), (2, 2)]


def gram_blocks(rows, part):
    for k, (a, b) in enumerate(PAIRS):
        block = lax.dot_general(
            rows[128 * a:128 * a + 128, :], rows[128 * b:128 * b + 128, :],
            (((1,), (1,)), ((), ())), precision=HIGH, preferred_element_type=F32)
        flat = k * 128
        while flat < k * 128 + 128:
            inside = flat % 24
            size = min(24 - inside, k * 128 + 128 - flat)
            slab = flat // 24
            part[slab // PLANE, slab % PLANE, inside:inside + size, :] = block[flat - k * 128:flat - k * 128 + size]
            flat += size


def field_kernel(cells, field, gram, send, send_sem, recv_sem, *sums):
    gx, gy, _, _, _ = position()
    barrier = pltpu.get_barrier_semaphore()
    loop(1, GX, lambda d: signal(barrier, ((gx + d) % GX, gy)))
    count = greet_sum(barrier)
    pl.semaphore_wait(barrier, GX - 1 + count)

    def turn(to):
        for k in range(6):
            start = pl.multiple_of(to * 64, 64)
            pair = [cells[2 * k + h, pl.ds(start, 64), :] for h in range(2)]
            yield slice(128 * k, 128 * k + 128), jnp.concatenate(pair, axis=0).T

    def copy(d):
        to = (gx + d) % GX
        return pltpu.make_async_remote_copy(
            src_ref=send.at[to], dst_ref=field.at[gx],
            send_sem=send_sem.at[d], recv_sem=recv_sem.at[d],
            device_id=(to, gy), device_id_type=MESH)

    def push(d):
        to = (gx + d) % GX
        for lanes, block in turn(to):
            send[to, :, lanes] = block
        copy(d).start()

    loop(1, GX, push)
    for lanes, block in turn(gx):
        field[gx, :, lanes] = block
    loop(1, GX, lambda d: copy(d).wait())
    gram_blocks(field[...].reshape(384, 768), sums[0])
    all_sum(sums[0], gram, *sums[1:])


def planes_kernel(reduced, rows, gram, send, planes, send_sem, recv_sem, *sums):
    gx, gy, _, _, _ = position()
    barrier = pltpu.get_barrier_semaphore()
    loop(1, GY, lambda d: signal(barrier, (gx, (gy + d) % GY)))
    count = greet_sum(barrier)
    pl.semaphore_wait(barrier, GY - 1 + count)

    for k in range(GY):
        send[k] = reduced[3 * k:3 * k + 3, :]

    def copy(d):
        to = (gy + d) % GY
        return pltpu.make_async_remote_copy(
            src_ref=send.at[to], dst_ref=planes.at[gy],
            send_sem=send_sem.at[d], recv_sem=recv_sem.at[d],
            device_id=(gx, to), device_id_type=MESH)

    loop(1, GY, lambda d: copy(d).start())
    planes[gy] = send[gy]
    loop(1, GY, lambda d: copy(d).wait())
    for y in range(12):
        parts = [planes[:, r, 64 * y:64 * y + 64] for r in range(3)]
        parts.append(jnp.zeros((GY, 64), F32))
        for k in range(2):
            rows[k, pl.ds(y, GY, stride=12), :] = jnp.concatenate(parts[2 * k:2 * k + 2], axis=1)
    gram_blocks(jnp.concatenate([rows[0], rows[1]], axis=1), sums[0])
    all_sum(sums[0], gram, *sums[1:])


def core_kernel(part, out, send, send_sem, recv_sem):
    gx, gy, _, _, _ = position()
    home = gy // 4
    slot = gx * 4 + gy % 4
    barrier = pltpu.get_barrier_semaphore()
    loop(0, GY, lambda k: signal(barrier, (k // 4, gx * 4 + k % 4)))
    pl.semaphore_wait(barrier, GY)

    for k in range(GY):
        send[k] = part[3 * k:3 * k + 3, :192]

    def copy(k):
        return pltpu.make_async_remote_copy(
            src_ref=send.at[k], dst_ref=out.at[slot],
            send_sem=send_sem.at[k], recv_sem=recv_sem.at[slot],
            device_id=(home, k), device_id_type=MESH)

    def arrival(k):
        return pltpu.make_async_remote_copy(
            src_ref=send.at[k], dst_ref=out.at[k],
            send_sem=send_sem.at[k], recv_sem=recv_sem.at[k],
            device_id=(home, k), device_id_type=MESH)

    def go(k):
        mine = (home == gx) & (k == gy)

        @pl.when(jnp.logical_not(mine))
        def _():
            copy(k).start()

        @pl.when(mine)
        def _():
            out[slot] = send[k]

    def finish(k):
        @pl.when(jnp.logical_not((home == gx) & (k == gy)))
        def _():
            copy(k).wait_send()

        @pl.when(jnp.logical_not((home == gx) & (k == slot)))
        def _():
            arrival(k).wait_recv()

    loop(0, GY, go)
    loop(0, GY, finish)


def params(number):
    return pltpu.CompilerParams(
        collective_id=number, has_side_effects=True, vmem_limit_bytes=40 * 1024 * 1024)


VM = pl.BlockSpec(memory_space=pltpu.VMEM)


def split(a):
    hi = a.astype(BF16)
    rest = a - hi.astype(F32)
    mid = rest.astype(BF16)
    return hi, mid, (rest - mid.astype(F32)).astype(BF16)


def dot(a, b, turned=False):
    dims = (((1,), (1 if turned else 0,)), ((), ()))

    def term(i, j):
        return lax.dot_general(a[i], b[j], dims, preferred_element_type=F32)

    small = term(0, 2) + term(2, 0) + term(1, 1)
    return term(0, 0) + (term(0, 1) + term(1, 0) + small)


def inverse_factor(cross, panel=16):
    rank = cross.shape[0]
    rows = lax.broadcasted_iota(jnp.int32, (panel, 128), 0)
    left = cross
    right = (lax.broadcasted_iota(jnp.int32, (rank, 128), 0)
             == lax.broadcasted_iota(jnp.int32, (rank, 128), 1)).astype(F32)
    outs = []
    for first in range(0, rank, panel):
        solved_left, solved_right, lower = left[:panel], right[:panel], right[:panel]
        columns = [
            jnp.broadcast_to(left[:panel, first + j:first + j + 1], (panel, 128)) for j in range(panel)]
        inverse = jnp.zeros((panel, 128), F32)
        for k in range(panel):
            pivot = 1.0 / jnp.broadcast_to(columns[k][k:k + 1], (panel, 128))
            ratio = columns[k] * pivot
            others = jnp.where(rows == k, 0.0, ratio)
            below = jnp.where(rows > k, ratio, 0.0)
            inverse = jnp.where(rows == k, pivot, inverse)
            for j in range(k + 1, panel):
                columns[j] = columns[j] - others * columns[j][k:k + 1]
            solved_left = solved_left - others * solved_left[k:k + 1]
            solved_right = solved_right - others * solved_right[k:k + 1]
            lower = lower - below * lower[k:k + 1]
        outs.append(lower * jnp.sqrt(inverse))
        if first + panel == rank:
            break
        solved = jnp.concatenate([solved_left * inverse, solved_right * inverse], axis=1)

        def place(block):
            parts = [block, jnp.zeros((128 - first - panel, 256), BF16)]
            if first:
                parts = [jnp.zeros((first, 256), BF16)] + parts
            return jnp.concatenate(parts, axis=0)

        high, mid, low = (place(t) for t in split(solved))
        a_high, a_mid, a_low = split(left[panel:])

        def wide(a, b, c, d):
            return jnp.dot(
                jnp.concatenate([a, b], axis=1), jnp.concatenate([c, d], axis=0),
                preferred_element_type=F32)

        update = wide(a_high, a_mid, high, high) + (
            wide(a_high, a_mid, mid, mid) + wide(a_high, a_low, low, high))
        left = left[panel:] - update[:, :128]
        right = right[panel:] - update[:, 128:]
    return jnp.concatenate(outs, axis=0)


def iterate(gram, start):
    blocks = gram.reshape(6, 128, 128)
    upper = {pair: blocks[k] for k, pair in enumerate(PAIRS)}
    full = jnp.concatenate([
        jnp.concatenate([upper[(a, b)] if a <= b else upper[(b, a)].T for b in range(3)], axis=1)
        for a in range(3)], axis=0)
    gram = split(full)
    own = start
    for _ in range(ITERS):
        image = dot(split(own), gram)
        image = jnp.concatenate([image, jnp.zeros((32, 384), F32)], axis=0)
        parts = split(image)
        cross = dot([t[:96] for t in parts], parts, turned=True)
        own = dot(split(inverse_factor(cross)), parts)
    return own


def own_rows(parts, first, count):
    row = lax.broadcasted_iota(jnp.int32, (count, 384), 0)
    pick = (lax.broadcasted_iota(jnp.int32, (count, 384), 1) == row + first).astype(BF16)
    dims = (((1,), (1,)), ((), ()))
    high, mid, low = (
        lax.dot_general(pick, t, dims, preferred_element_type=F32) for t in parts)
    return high + mid + low


def basis_x_kernel(gram, start, field, own, reduced):
    parts = split(iterate(gram[...], start[...]))
    own[...] = own_rows(parts, lax.axis_index("gx") * 48, 48)
    reduced[...] = dot(parts, split(field[...].reshape(384, 768)))


def basis_y_kernel(gram, start, rows, own, core):
    parts = split(iterate(gram[...], start[...]))
    own[...] = own_rows(parts, lax.axis_index("gy") * 12, 12)
    core[...] = dot(parts, split(jnp.concatenate([rows[0], rows[1]], axis=1)))


def compute(body, out, name):
    return pl.pallas_call(
        body,
        out_shape=[jax.ShapeDtypeStruct(shape, F32) for shape in out],
        in_specs=[VM] * 3,
        out_specs=[VM] * 2,
        compiler_params=pltpu.CompilerParams(vmem_limit_bytes=40 * 1024 * 1024),
        name=name,
    )


def local(snapshot, start_x, start_y):
    cells = jnp.transpose(snapshot, (1, 2, 3, 0)).reshape(12, 512, 48)
    field, gram_x = pl.pallas_call(
        field_kernel,
        out_shape=[
            jax.ShapeDtypeStruct((GX, 48, 768), F32),
            jax.ShapeDtypeStruct((2, PLANE, 24, 128), F32),
        ],
        in_specs=[VM],
        out_specs=[VM, VM],
        scratch_shapes=[
            pltpu.VMEM((GX, 48, 768), F32),
            pltpu.SemaphoreType.DMA((GX,)),
            pltpu.SemaphoreType.DMA((GX,)),
        ] + sum_scratch(),
        compiler_params=params(1),
        name="field",
    )(cells)
    own_x, reduced = compute(basis_x_kernel, [(48, 96), (96, 768)], "basis_x")(gram_x, start_x.T, field)
    rows, gram_y = pl.pallas_call(
        planes_kernel,
        out_shape=[
            jax.ShapeDtypeStruct((2, 384, 128), F32),
            jax.ShapeDtypeStruct((2, PLANE, 24, 128), F32),
        ],
        in_specs=[VM],
        out_specs=[VM, VM],
        scratch_shapes=[
            pltpu.VMEM((GY, 3, 768), F32),
            pltpu.VMEM((GY, 3, 768), F32),
            pltpu.SemaphoreType.DMA((GY,)),
            pltpu.SemaphoreType.DMA((GY,)),
        ] + sum_scratch(),
        compiler_params=params(2),
        name="planes",
    )(reduced)
    own_y, core = compute(basis_y_kernel, [(12, 96), (96, 256)], "basis_y")(gram_y, start_y.T, rows)
    pieces = pl.pallas_call(
        core_kernel,
        out_shape=jax.ShapeDtypeStruct((GY, 3, 192), F32),
        in_specs=[VM],
        out_specs=VM,
        scratch_shapes=[
            pltpu.VMEM((GY, 3, 192), F32),
            pltpu.SemaphoreType.DMA((GY,)),
            pltpu.SemaphoreType.DMA((GY,)),
        ],
        compiler_params=params(3),
        name="core",
    )(core)
    pieces = pieces.reshape(8, 4, 3, 3, 4, 16)
    core = jnp.transpose(pieces, (1, 3, 2, 0, 4, 5)).reshape(12, 3, 32, 16)
    return (own_x, own_y, core)


def solution(mesh):
    in_specs = (P("gx", "gy", None, None), P(), P())
    out_specs = (P("gx", None), P("gy", None), P("gx", "gy", None, None))
    return jax.shard_map(local, mesh=mesh, in_specs=in_specs, out_specs=out_specs, check_vma=False)
```

```python
import jax
import jax.numpy as jnp
from jax import lax
from jax.experimental import pallas as pl
from jax.experimental.pallas import tpu as pltpu
from jax.sharding import PartitionSpec as P

ITERS = 4
HIGH = lax.Precision.HIGHEST
MESH = pl.DeviceIdType.MESH
F32 = jnp.float32
BF16 = jnp.bfloat16

NXC, NYC, NZC = 4, 4, 8
GX, GY = 8, 32
PLANE = NXC * NYC


def position():
    gx, gy = lax.axis_index("gx"), lax.axis_index("gy")
    z = (gy // 8) * 2 + gx // 4
    plane = ((gy // 2) % 4) * 4 + gx % 4
    return gx, gy, z, plane, gy % 2


def device(z, plane, core):
    return ((z % 2) * 4 + plane % 4, (z // 2) * 8 + (plane // 4) * 2 + core)


def loop(low, high, body):
    def step(i, carry):
        body(i)
        return carry

    lax.fori_loop(low, high, step, 0)


def signal(sem, where):
    pl.semaphore_signal(sem, inc=1, device_id=where, device_id_type=MESH)


def sum_scratch():
    return [
        pltpu.VMEM((2, PLANE, 24, 128), F32),
        pltpu.VMEM((2, PLANE, 24, 128), F32),
        pltpu.VMEM((PLANE, 24, 128), F32),
        pltpu.VMEM((PLANE, 24, 128), F32),
        pltpu.VMEM((NZC, 24, 128), F32),
        pltpu.SemaphoreType.DMA((2, 2)),
        pltpu.SemaphoreType.DMA((2, 2, PLANE)),
        pltpu.SemaphoreType.DMA((2, NZC)),
    ]


def all_sum(part, out, half, slots, zslots, core_sem, plane_sem, z_sem):
    _, _, z, plane, core = position()

    def core_copy(src, dst, k):
        return pltpu.make_async_remote_copy(
            src_ref=src, dst_ref=dst, send_sem=core_sem.at[k, 0], recv_sem=core_sem.at[k, 1],
            device_id=device(z, plane, 1 - core), device_id_type=MESH)

    copy = core_copy(part.at[1 - core], half, 0)
    copy.start()
    copy.wait()
    half[...] += part[core]

    def scatter(d):
        to = (plane + d) % PLANE
        return pltpu.make_async_remote_copy(
            src_ref=half.at[to], dst_ref=slots.at[d],
            send_sem=plane_sem.at[0, 0, d], recv_sem=plane_sem.at[0, 1, d],
            device_id=device(z, to, core), device_id_type=MESH)

    loop(1, PLANE, lambda d: scatter(d).start())
    loop(1, PLANE, lambda d: scatter(d).wait())
    total = half[plane]
    for d in range(1, PLANE):
        total += slots[d]
    zslots[z] = total

    def spread(d):
        return pltpu.make_async_remote_copy(
            src_ref=zslots.at[z], dst_ref=zslots.at[z],
            send_sem=z_sem.at[0, d], recv_sem=z_sem.at[1, d],
            device_id=device((z + d) % NZC, plane, core), device_id_type=MESH)

    loop(1, NZC, lambda d: spread(d).start())
    loop(1, NZC, lambda d: spread(d).wait())
    total = zslots[0]
    for k in range(1, NZC):
        total += zslots[k]
    out[core, plane] = total

    def gather(d):
        return pltpu.make_async_remote_copy(
            src_ref=out.at[core, plane], dst_ref=out.at[core, plane],
            send_sem=plane_sem.at[1, 0, d], recv_sem=plane_sem.at[1, 1, d],
            device_id=device(z, (plane + d) % PLANE, core), device_id_type=MESH)

    loop(1, PLANE, lambda d: gather(d).start())
    loop(1, PLANE, lambda d: gather(d).wait())
    copy = core_copy(out.at[core], out.at[core], 1)
    copy.start()
    copy.wait()


PAIRS = [(0, 0), (0, 1), (0, 2), (1, 1), (1, 2), (2, 2)]


def gram_blocks(rows, part):
    for k, (a, b) in enumerate(PAIRS):
        block = lax.dot_general(
            rows[128 * a:128 * a + 128, :], rows[128 * b:128 * b + 128, :],
            (((1,), (1,)), ((), ())), precision=HIGH, preferred_element_type=F32)
        flat = k * 128
        while flat < k * 128 + 128:
            inside = flat % 24
            size = min(24 - inside, k * 128 + 128 - flat)
            slab = flat // 24
            part[slab // PLANE, slab % PLANE, inside:inside + size, :] = block[flat - k * 128:flat - k * 128 + size]
            flat += size


def split(a):
    hi = a.astype(BF16)
    rest = a - hi.astype(F32)
    mid = rest.astype(BF16)
    return hi, mid, (rest - mid.astype(F32)).astype(BF16)


def dot(a, b, turned=False):
    dims = (((1,), (1 if turned else 0,)), ((), ()))

    def term(i, j):
        return lax.dot_general(a[i], b[j], dims, preferred_element_type=F32)

    small = term(0, 2) + term(2, 0) + term(1, 1)
    return term(0, 0) + (term(0, 1) + term(1, 0) + small)


def inverse_factor(cross, panel=16):
    rank = cross.shape[0]
    rows = lax.broadcasted_iota(jnp.int32, (panel, 128), 0)
    left = cross
    right = (lax.broadcasted_iota(jnp.int32, (rank, 128), 0)
             == lax.broadcasted_iota(jnp.int32, (rank, 128), 1)).astype(F32)
    outs = []
    for first in range(0, rank, panel):
        solved_left, solved_right, lower = left[:panel], right[:panel], right[:panel]
        columns = [
            jnp.broadcast_to(left[:panel, first + j:first + j + 1], (panel, 128)) for j in range(panel)]
        inverse = jnp.zeros((panel, 128), F32)
        for k in range(panel):
            pivot = 1.0 / jnp.broadcast_to(columns[k][k:k + 1], (panel, 128))
            ratio = columns[k] * pivot
            others = jnp.where(rows == k, 0.0, ratio)
            below = jnp.where(rows > k, ratio, 0.0)
            inverse = jnp.where(rows == k, pivot, inverse)
            for j in range(k + 1, panel):
                columns[j] = columns[j] - others * columns[j][k:k + 1]
            solved_left = solved_left - others * solved_left[k:k + 1]
            solved_right = solved_right - others * solved_right[k:k + 1]
            lower = lower - below * lower[k:k + 1]
        outs.append(lower * jnp.sqrt(inverse))
        if first + panel == rank:
            break
        solved = jnp.concatenate([solved_left * inverse, solved_right * inverse], axis=1)

        def place(block):
            parts = [block, jnp.zeros((128 - first - panel, 256), BF16)]
            if first:
                parts = [jnp.zeros((first, 256), BF16)] + parts
            return jnp.concatenate(parts, axis=0)

        high, mid, low = (place(t) for t in split(solved))
        a_high, a_mid, a_low = split(left[panel:])

        def wide(a, b, c, d):
            return jnp.dot(
                jnp.concatenate([a, b], axis=1), jnp.concatenate([c, d], axis=0),
                preferred_element_type=F32)

        update = wide(a_high, a_mid, high, high) + (
            wide(a_high, a_mid, mid, mid) + wide(a_high, a_low, low, high))
        left = left[panel:] - update[:, :128]
        right = right[panel:] - update[:, 128:]
    return jnp.concatenate(outs, axis=0)


def iterate(packed, start, gram, own):
    blocks = packed[...].reshape(6, 128, 128)
    upper = {pair: blocks[k] for k, pair in enumerate(PAIRS)}
    full = jnp.concatenate([
        jnp.concatenate([upper[(a, b)] if a <= b else upper[(b, a)].T for b in range(3)], axis=1)
        for a in range(3)], axis=0)
    for k, term in enumerate(split(full)):
        gram[k] = term
    own[...] = start[...]

    def step(_):
        image = dot(split(own[...]), [gram[k] for k in range(3)])
        image = jnp.concatenate([image, jnp.zeros((32, 384), F32)], axis=0)
        parts = split(image)
        cross = dot([t[:96] for t in parts], parts, turned=True)
        own[...] = dot(split(inverse_factor(cross)), parts)

    loop(0, ITERS, step)


def own_rows(parts, first, count):
    row = lax.broadcasted_iota(jnp.int32, (count, 384), 0)
    pick = (lax.broadcasted_iota(jnp.int32, (count, 384), 1) == row + first).astype(BF16)
    dims = (((1,), (1,)), ((), ()))
    high, mid, low = (
        lax.dot_general(pick, t, dims, preferred_element_type=F32) for t in parts)
    return high + mid + low


def greet(barrier):
    gx, gy, z, plane, core = position()
    loop(1, GX, lambda d: signal(barrier, ((gx + d) % GX, gy)))
    signal(barrier, device(z, plane, 1 - core))
    loop(1, PLANE, lambda d: signal(barrier, device(z, (plane + d) % PLANE, core)))
    loop(1, NZC, lambda d: signal(barrier, device((z + d) % NZC, plane, core)))
    loop(1, GY, lambda d: signal(barrier, (gx, (gy + d) % GY)))
    loop(0, GY, lambda k: signal(barrier, (k // 4, gx * 4 + k % 4)))
    return GX - 1 + 1 + PLANE - 1 + NZC - 1 + GY - 1 + GY


def window_kernel(cells, start_x, start_y, own_x, own_y, out, send_x, field, send_y, planes, rows, send_c,
                  basis, gram, sem_x, sem_y, sem_c, *sums):
    gx, gy, _, _, _ = position()
    sums_x, sums_y = sums[:len(sums) // 2], sums[len(sums) // 2:]
    barrier = pltpu.get_barrier_semaphore()
    count = greet(barrier)

    def turn(to):
        for k in range(6):
            start = pl.multiple_of(to * 64, 64)
            pair = [cells[2 * k + h, pl.ds(start, 64), :] for h in range(2)]
            yield slice(128 * k, 128 * k + 128), jnp.concatenate(pair, axis=0).T

    def push_x(d):
        to = (gx + d) % GX
        for lanes, block in turn(to):
            send_x[to, :, lanes] = block

    def copy_x(d):
        to = (gx + d) % GX
        return pltpu.make_async_remote_copy(
            src_ref=send_x.at[to], dst_ref=field.at[gx],
            send_sem=sem_x.at[0, d], recv_sem=sem_x.at[1, d],
            device_id=(to, gy), device_id_type=MESH)

    loop(1, GX, push_x)
    for lanes, block in turn(gx):
        field[gx, :, lanes] = block
    pl.semaphore_wait(barrier, count)
    loop(1, GX, lambda d: copy_x(d).start())
    loop(1, GX, lambda d: copy_x(d).wait())
    gram_blocks(field[...].reshape(384, 768), sums_x[0])
    all_sum(*sums_x)
    iterate(sums_x[1], start_x, gram, basis)
    parts = split(basis[...])
    own_x[...] = own_rows(parts, gx * 48, 48)

    reduced = dot(parts, split(field[...].reshape(384, 768)))
    for k in range(GY):
        send_y[k] = reduced[3 * k:3 * k + 3, :]

    def copy_y(d):
        to = (gy + d) % GY
        return pltpu.make_async_remote_copy(
            src_ref=send_y.at[to], dst_ref=planes.at[gy],
            send_sem=sem_y.at[0, d], recv_sem=sem_y.at[1, d],
            device_id=(gx, to), device_id_type=MESH)

    loop(1, GY, lambda d: copy_y(d).start())
    planes[gy] = send_y[gy]
    loop(1, GY, lambda d: copy_y(d).wait())
    for y in range(12):
        pieces = [planes[:, r, 64 * y:64 * y + 64] for r in range(3)]
        pieces.append(jnp.zeros((GY, 64), F32))
        for k in range(2):
            rows[k, pl.ds(y, GY, stride=12), :] = jnp.concatenate(pieces[2 * k:2 * k + 2], axis=1)
    gram_blocks(jnp.concatenate([rows[0], rows[1]], axis=1), sums_y[0])
    all_sum(*sums_y)
    iterate(sums_y[1], start_y, gram, basis)
    parts = split(basis[...])
    own_y[...] = own_rows(parts, gy * 12, 12)

    core = dot(parts, split(jnp.concatenate([rows[0], rows[1]], axis=1)))
    for k in range(GY):
        send_c[k] = core[3 * k:3 * k + 3, :192]
    home = gy // 4
    slot = gx * 4 + gy % 4

    def copy_c(k, to):
        return pltpu.make_async_remote_copy(
            src_ref=send_c.at[k], dst_ref=out.at[to],
            send_sem=sem_c.at[0, k], recv_sem=sem_c.at[1, to],
            device_id=(home, k), device_id_type=MESH)

    def go(k):
        mine = (home == gx) & (k == gy)

        @pl.when(jnp.logical_not(mine))
        def _():
            copy_c(k, slot).start()

        @pl.when(mine)
        def _():
            out[slot] = send_c[k]

    def finish(k):
        @pl.when(jnp.logical_not((home == gx) & (k == gy)))
        def _():
            copy_c(k, slot).wait_send()

        @pl.when(jnp.logical_not((home == gx) & (k == slot)))
        def _():
            copy_c(k, k).wait_recv()

    loop(0, GY, go)
    loop(0, GY, finish)


VM = pl.BlockSpec(memory_space=pltpu.VMEM)


def local(snapshot, start_x, start_y):
    cells = jnp.transpose(snapshot, (1, 2, 3, 0)).reshape(12, 512, 48)
    own_x, own_y, pieces = pl.pallas_call(
        window_kernel,
        out_shape=[jax.ShapeDtypeStruct(shape, F32) for shape in ((48, 96), (12, 96), (GY, 3, 192))],
        in_specs=[VM] * 3,
        out_specs=[VM] * 3,
        scratch_shapes=[
            pltpu.VMEM((GX, 48, 768), F32),
            pltpu.VMEM((GX, 48, 768), F32),
            pltpu.VMEM((GY, 3, 768), F32),
            pltpu.VMEM((GY, 3, 768), F32),
            pltpu.VMEM((2, 384, 128), F32),
            pltpu.VMEM((GY, 3, 192), F32),
            pltpu.VMEM((96, 384), F32),
            pltpu.VMEM((3, 384, 384), BF16),
            pltpu.SemaphoreType.DMA((2, GX)),
            pltpu.SemaphoreType.DMA((2, GY)),
            pltpu.SemaphoreType.DMA((2, GY)),
        ] + sum_scratch() + sum_scratch(),
        compiler_params=pltpu.CompilerParams(
            collective_id=1, has_side_effects=True, vmem_limit_bytes=48 * 1024 * 1024),
        name="window",
    )(cells, start_x.T, start_y.T)
    pieces = pieces.reshape(8, 4, 3, 3, 4, 16)
    core = jnp.transpose(pieces, (1, 3, 2, 0, 4, 5)).reshape(12, 3, 32, 16)
    return (own_x, own_y, core)


def solution(mesh):
    in_specs = (P("gx", "gy", None, None), P(), P())
    out_specs = (P("gx", None), P("gy", None), P("gx", "gy", None, None))
    return jax.shard_map(local, mesh=mesh, in_specs=in_specs, out_specs=out_specs, check_vma=False)
```

```python
import jax
import jax.numpy as jnp
from jax import lax
from jax.experimental import pallas as pl
from jax.experimental.pallas import tpu as pltpu
from jax.sharding import PartitionSpec as P

ITERS = 4
MESH = pl.DeviceIdType.MESH
F32 = jnp.float32
BF16 = jnp.bfloat16

NXC, NYC, NZC = 4, 4, 8
GX, GY = 8, 32
CHUNKS = 3
PLANE = NXC * NYC


def position():
    gx, gy = lax.axis_index("gx"), lax.axis_index("gy")
    z = (gy // 8) * 2 + gx // 4
    plane = ((gy // 2) % 4) * 4 + gx % 4
    return gx, gy, z, plane, gy % 2


def device(z, plane, core):
    return ((z % 2) * 4 + plane % 4, (z // 2) * 8 + (plane // 4) * 2 + core)


def loop(low, high, body):
    def step(i, carry):
        body(i)
        return carry

    lax.fori_loop(low, high, step, 0)


def signal(sem, where):
    pl.semaphore_signal(sem, inc=1, device_id=where, device_id_type=MESH)


def sum_scratch():
    return [
        pltpu.VMEM((2, PLANE, 24, 128), F32),
        pltpu.VMEM((2, PLANE, 24, 128), F32),
        pltpu.VMEM((PLANE, 24, 128), F32),
        pltpu.VMEM((PLANE, 24, 128), F32),
        pltpu.VMEM((NZC, 24, 128), F32),
        pltpu.SemaphoreType.DMA((1 + PLANE, 2)),
        pltpu.SemaphoreType.DMA((2, 2, PLANE)),
        pltpu.SemaphoreType.DMA((2, NZC)),
    ]


def all_sum(part, out, half, slots, zslots, core_sem, plane_sem, z_sem):
    _, _, z, plane, core = position()

    def core_copy(src, dst, k):
        return pltpu.make_async_remote_copy(
            src_ref=src, dst_ref=dst, send_sem=core_sem.at[k, 0], recv_sem=core_sem.at[k, 1],
            device_id=device(z, plane, 1 - core), device_id_type=MESH)

    copy = core_copy(part.at[1 - core], half, 0)
    copy.start()
    copy.wait()
    half[...] += part[core]

    def scatter(d):
        to = (plane + d) % PLANE
        return pltpu.make_async_remote_copy(
            src_ref=half.at[to], dst_ref=slots.at[d],
            send_sem=plane_sem.at[0, 0, d], recv_sem=plane_sem.at[0, 1, d],
            device_id=device(z, to, core), device_id_type=MESH)

    loop(1, PLANE, lambda d: scatter(d).start())
    loop(1, PLANE, lambda d: scatter(d).wait())
    total = half[plane]
    for d in range(1, PLANE):
        total += slots[d]
    zslots[z] = total

    def spread(d):
        return pltpu.make_async_remote_copy(
            src_ref=zslots.at[z], dst_ref=zslots.at[z],
            send_sem=z_sem.at[0, d], recv_sem=z_sem.at[1, d],
            device_id=device((z + d) % NZC, plane, core), device_id_type=MESH)

    loop(1, NZC, lambda d: spread(d).start())
    loop(1, NZC, lambda d: spread(d).wait())
    total = zslots[0]
    for k in range(1, NZC):
        total += zslots[k]
    out[core, plane] = total

    def gather(d):
        return pltpu.make_async_remote_copy(
            src_ref=out.at[core, plane], dst_ref=out.at[core, plane],
            send_sem=plane_sem.at[1, 0, d], recv_sem=plane_sem.at[1, 1, d],
            device_id=device(z, (plane + d) % PLANE, core), device_id_type=MESH)

    def forward(k):
        return core_copy(out.at[core, k], out.at[core, k], 1 + k)

    loop(1, PLANE, lambda d: gather(d).start())
    forward(plane).start()

    def pass_on(d):
        gather(d).wait_recv()
        forward((plane + PLANE - d) % PLANE).start()

    loop(1, PLANE, pass_on)
    loop(1, PLANE, lambda d: gather(d).wait_send())
    loop(0, PLANE, lambda k: forward(k).wait())


PAIRS = [(0, 0), (0, 1), (0, 2), (1, 1), (1, 2), (2, 2)]


def split(a):
    hi = a.astype(BF16)
    rest = a - hi.astype(F32)
    mid = rest.astype(BF16)
    return hi, mid, (rest - mid.astype(F32)).astype(BF16)


def dot(a, b, turned=False):
    dims = (((1,), (1 if turned else 0,)), ((), ()))

    def term(i, j):
        return lax.dot_general(a[i], b[j], dims, preferred_element_type=F32)

    small = term(0, 2) + term(2, 0) + term(1, 1)
    return term(0, 0) + (term(0, 1) + term(1, 0) + small)


def gram_terms(rows):
    high, mid, low = split(rows)

    def term(a, b):
        return lax.dot_general(a, b, (((1,), (1,)), ((), ())), preferred_element_type=F32)

    return term(high, high) + term(mid, mid), term(high, mid) + term(high, low)


def store_blocks(full, part):
    for k, (a, b) in enumerate(PAIRS):
        flat = k * 128
        while flat < k * 128 + 128:
            inside = flat % 24
            size = min(24 - inside, k * 128 + 128 - flat)
            slab = flat // 24
            row = 128 * a + flat - k * 128
            part[slab // PLANE, slab % PLANE, inside:inside + size, :] = full[row:row + size, 128 * b:128 * b + 128]
            flat += size


def inverse_factor(cross, panel=16):
    rank = cross.shape[0]
    rows = lax.broadcasted_iota(jnp.int32, (panel, 128), 0)
    left = cross
    right = (lax.broadcasted_iota(jnp.int32, (rank, 128), 0)
             == lax.broadcasted_iota(jnp.int32, (rank, 128), 1)).astype(F32)
    outs = []
    for first in range(0, rank, panel):
        solved_left, solved_right, lower = left[:panel], right[:panel], right[:panel]
        columns = [
            jnp.broadcast_to(left[:panel, first + j:first + j + 1], (panel, 128)) for j in range(panel)]
        inverse = jnp.zeros((panel, 128), F32)
        for k in range(panel):
            pivot = 1.0 / jnp.broadcast_to(columns[k][k:k + 1], (panel, 128))
            ratio = columns[k] * pivot
            others = jnp.where(rows == k, 0.0, ratio)
            below = jnp.where(rows > k, ratio, 0.0)
            inverse = jnp.where(rows == k, pivot, inverse)
            for j in range(k + 1, panel):
                columns[j] = columns[j] - others * columns[j][k:k + 1]
            solved_left = solved_left - others * solved_left[k:k + 1]
            solved_right = solved_right - others * solved_right[k:k + 1]
            lower = lower - below * lower[k:k + 1]
        outs.append(lower * jnp.sqrt(inverse))
        if first + panel == rank:
            break
        solved = jnp.concatenate([solved_left * inverse, solved_right * inverse], axis=1)

        def place(block):
            parts = [block, jnp.zeros((128 - first - panel, 256), BF16)]
            if first:
                parts = [jnp.zeros((first, 256), BF16)] + parts
            return jnp.concatenate(parts, axis=0)

        high, mid, low = (place(t) for t in split(solved))
        a_high, a_mid, a_low = split(left[panel:])

        def wide(a, b, c, d):
            return jnp.dot(
                jnp.concatenate([a, b], axis=1), jnp.concatenate([c, d], axis=0),
                preferred_element_type=F32)

        update = wide(a_high, a_mid, high, high) + (
            wide(a_high, a_mid, mid, mid) + wide(a_high, a_low, low, high))
        left = left[panel:] - update[:, :128]
        right = right[panel:] - update[:, 128:]
    return jnp.concatenate(outs, axis=0)


def iterate(packed, start, gram, own):
    blocks = packed[...].reshape(6, 128, 128)
    upper = {pair: blocks[k] for k, pair in enumerate(PAIRS)}
    full = jnp.concatenate([
        jnp.concatenate([upper[(a, b)] if a <= b else upper[(b, a)].T for b in range(3)], axis=1)
        for a in range(3)], axis=0)
    for k, term in enumerate(split(full)):
        gram[k] = term
    own[...] = start[...]

    def step(_):
        image = dot(split(own[...]), [gram[k] for k in range(3)])
        image = jnp.concatenate([image, jnp.zeros((32, 384), F32)], axis=0)
        parts = split(image)
        cross = dot([t[:96] for t in parts], parts, turned=True)
        own[...] = dot(split(inverse_factor(cross)), parts)

    loop(0, ITERS, step)


def own_rows(parts, first, count):
    row = lax.broadcasted_iota(jnp.int32, (count, 384), 0)
    pick = (lax.broadcasted_iota(jnp.int32, (count, 384), 1) == row + first).astype(BF16)
    dims = (((1,), (1,)), ((), ()))
    high, mid, low = (
        lax.dot_general(pick, t, dims, preferred_element_type=F32) for t in parts)
    return high + mid + low


def greet(barrier):
    gx, gy, z, plane, core = position()
    loop(1, GX, lambda d: signal(barrier, ((gx + d) % GX, gy)))
    signal(barrier, device(z, plane, 1 - core))
    loop(1, PLANE, lambda d: signal(barrier, device(z, (plane + d) % PLANE, core)))
    loop(1, NZC, lambda d: signal(barrier, device((z + d) % NZC, plane, core)))
    return GX - 1 + 1 + PLANE - 1 + NZC - 1


def window_kernel(cells_hbm, start_x_hbm, start_y_hbm, own_x, own_y, out, cells, start_x, start_y, send_x, field,
                  send_y, planes, rows, send_c, basis, gram, sem_in, sem_x, sem_y, sem_c, *sums):
    gx, gy, _, _, _ = position()
    sums_x, sums_y = sums[:len(sums) // 2], sums[len(sums) // 2:]

    def fetch(h):
        return pltpu.make_async_copy(cells_hbm.at[pl.ds(4 * h, 4)], cells.at[pl.ds(4 * h, 4)], sem_in.at[h])

    starts = [
        pltpu.make_async_copy(start_x_hbm, start_x, sem_in.at[CHUNKS]),
        pltpu.make_async_copy(start_y_hbm, start_y, sem_in.at[CHUNKS + 1])]
    for h in range(CHUNKS):
        fetch(h).start()
    for start in starts:
        start.start()
    barrier = pltpu.get_barrier_semaphore()
    count = greet(barrier)

    def turn(h, to, target):
        first = pl.multiple_of(to * 64, 64)
        for k in range(2):
            pair = [cells[4 * h + 2 * k + i, pl.ds(first, 64), :] for i in range(2)]
            target[:, 128 * k:128 * k + 128] = jnp.concatenate(pair, axis=0).T

    def copy_x(h, d):
        to = (gx + d) % GX
        return pltpu.make_async_remote_copy(
            src_ref=send_x.at[h, to], dst_ref=field.at[h, gx],
            send_sem=sem_x.at[0, h, d], recv_sem=sem_x.at[1, h, d],
            device_id=(to, gy), device_id_type=MESH)

    for h in range(CHUNKS):
        fetch(h).wait()
        loop(1, GX, lambda d: turn(h, (gx + d) % GX, send_x.at[h, (gx + d) % GX]))
        if h == 0:
            pl.semaphore_wait(barrier, count)
        loop(1, GX, lambda d: copy_x(h, d).start())
    for h in range(CHUNKS):
        turn(h, gx, field.at[h, gx])
    straight, crossed = 0.0, 0.0
    for h in range(CHUNKS):
        loop(1, GX, lambda d: copy_x(h, d).wait_recv())
        terms = gram_terms(field[h].reshape(384, 256))
        straight, crossed = straight + terms[0], crossed + terms[1]
    store_blocks(straight + (crossed + crossed.T), sums_x[0])
    all_sum(*sums_x)
    for h in range(CHUNKS):
        loop(1, GX, lambda d: copy_x(h, d).wait_send())
    for start in starts:
        start.wait()
    iterate(sums_x[1], start_x, gram, basis)
    parts = split(basis[...])
    own_x[...] = own_rows(parts, gx * 48, 48)

    for h in range(CHUNKS):
        reduced = dot(parts, split(field[h].reshape(384, 256)))
        for k in range(GY):
            send_y[k, :, 256 * h:256 * h + 256] = reduced[3 * k:3 * k + 3, :]

    def copy_y(d):
        to = (gy + d) % GY
        return pltpu.make_async_remote_copy(
            src_ref=send_y.at[to], dst_ref=planes.at[gy],
            send_sem=sem_y.at[0, d], recv_sem=sem_y.at[1, d],
            device_id=(gx, to), device_id_type=MESH)

    loop(1, GY, lambda d: copy_y(d).start())
    planes[gy] = send_y[gy]
    loop(1, GY, lambda d: copy_y(d).wait())
    for y in range(12):
        pieces = [planes[:, r, 64 * y:64 * y + 64] for r in range(3)]
        pieces.append(jnp.zeros((GY, 64), F32))
        for k in range(2):
            rows[k, pl.ds(y, GY, stride=12), :] = jnp.concatenate(pieces[2 * k:2 * k + 2], axis=1)
    straight, crossed = gram_terms(jnp.concatenate([rows[0], rows[1]], axis=1))
    store_blocks(straight + (crossed + crossed.T), sums_y[0])
    all_sum(*sums_y)
    iterate(sums_y[1], start_y, gram, basis)
    parts = split(basis[...])
    own_y[...] = own_rows(parts, gy * 12, 12)

    core = dot(parts, split(jnp.concatenate([rows[0], rows[1]], axis=1)))
    for k in range(GY):
        send_c[k] = core[3 * k:3 * k + 3, :192]
    home = gy // 4
    slot = gx * 4 + gy % 4

    def copy_c(k, to):
        return pltpu.make_async_remote_copy(
            src_ref=send_c.at[k], dst_ref=out.at[to],
            send_sem=sem_c.at[0, k], recv_sem=sem_c.at[1, to],
            device_id=(home, k), device_id_type=MESH)

    def go(k):
        mine = (home == gx) & (k == gy)

        @pl.when(jnp.logical_not(mine))
        def _():
            copy_c(k, slot).start()

        @pl.when(mine)
        def _():
            out[slot] = send_c[k]

    def finish(k):
        @pl.when(jnp.logical_not((home == gx) & (k == gy)))
        def _():
            copy_c(k, slot).wait_send()

        @pl.when(jnp.logical_not((home == gx) & (k == slot)))
        def _():
            copy_c(k, k).wait_recv()

    loop(0, GY, go)
    loop(0, GY, finish)


VM = pl.BlockSpec(memory_space=pltpu.VMEM)


def local(snapshot, start_x, start_y):
    cells = jnp.transpose(snapshot, (1, 2, 3, 0)).reshape(12, 512, 48)
    own_x, own_y, pieces = pl.pallas_call(
        window_kernel,
        out_shape=[jax.ShapeDtypeStruct(shape, F32) for shape in ((48, 96), (12, 96), (GY, 3, 192))],
        in_specs=[pl.BlockSpec(memory_space=pltpu.HBM)] * 3,
        out_specs=[VM] * 3,
        scratch_shapes=[
            pltpu.VMEM((12, 512, 48), F32),
            pltpu.VMEM((96, 384), F32),
            pltpu.VMEM((96, 384), F32),
            pltpu.VMEM((CHUNKS, GX, 48, 256), F32),
            pltpu.VMEM((CHUNKS, GX, 48, 256), F32),
            pltpu.VMEM((GY, 3, 768), F32),
            pltpu.VMEM((GY, 3, 768), F32),
            pltpu.VMEM((2, 384, 128), F32),
            pltpu.VMEM((GY, 3, 192), F32),
            pltpu.VMEM((96, 384), F32),
            pltpu.VMEM((3, 384, 384), BF16),
            pltpu.SemaphoreType.DMA((CHUNKS + 2,)),
            pltpu.SemaphoreType.DMA((2, CHUNKS, GX)),
            pltpu.SemaphoreType.DMA((2, GY)),
            pltpu.SemaphoreType.DMA((2, GY)),
        ] + sum_scratch() + sum_scratch(),
        compiler_params=pltpu.CompilerParams(
            collective_id=1, has_side_effects=True, vmem_limit_bytes=48 * 1024 * 1024),
        name="window",
    )(cells, start_x.T, start_y.T)
    pieces = pieces.reshape(8, 4, 3, 3, 4, 16)
    core = jnp.transpose(pieces, (1, 3, 2, 0, 4, 5)).reshape(12, 3, 32, 16)
    return (own_x, own_y, core)


def solution(mesh):
    in_specs = (P("gx", "gy", None, None), P(), P())
    out_specs = (P("gx", None), P("gy", None), P("gx", "gy", None, None))
    return jax.shard_map(local, mesh=mesh, in_specs=in_specs, out_specs=out_specs, check_vma=False)
```

```python
import jax
import jax.numpy as jnp
from jax import lax
from jax.experimental import pallas as pl
from jax.experimental.pallas import tpu as pltpu
from jax.sharding import PartitionSpec as P

ITERS = 4
MESH = pl.DeviceIdType.MESH
F32 = jnp.float32
BF16 = jnp.bfloat16

NXC, NYC, NZC = 4, 4, 8
GX, GY = 8, 32
CHUNKS = 3
PLANE = NXC * NYC


def position():
    gx, gy = lax.axis_index("gx"), lax.axis_index("gy")
    z = (gy // 8) * 2 + gx // 4
    plane = ((gy // 2) % 4) * 4 + gx % 4
    return gx, gy, z, plane, gy % 2


def device(z, plane, core):
    return ((z % 2) * 4 + plane % 4, (z // 2) * 8 + (plane // 4) * 2 + core)


def loop(low, high, body):
    def step(i, carry):
        body(i)
        return carry

    lax.fori_loop(low, high, step, 0)


def signal(sem, where):
    pl.semaphore_signal(sem, inc=1, device_id=where, device_id_type=MESH)


def sum_scratch():
    return [
        pltpu.VMEM((2, PLANE, 24, 128), F32),
        pltpu.VMEM((2, PLANE, 24, 128), F32),
        pltpu.VMEM((PLANE, 24, 128), F32),
        pltpu.VMEM((PLANE, 24, 128), F32),
        pltpu.VMEM((NZC, 24, 128), F32),
        pltpu.SemaphoreType.DMA((1 + PLANE, 2)),
        pltpu.SemaphoreType.DMA((2, 2, PLANE)),
        pltpu.SemaphoreType.DMA((2, NZC)),
    ]


def all_sum(part, out, half, slots, zslots, core_sem, plane_sem, z_sem):
    _, _, z, plane, core = position()

    def core_copy(src, dst, k):
        return pltpu.make_async_remote_copy(
            src_ref=src, dst_ref=dst, send_sem=core_sem.at[k, 0], recv_sem=core_sem.at[k, 1],
            device_id=device(z, plane, 1 - core), device_id_type=MESH)

    copy = core_copy(part.at[1 - core], half, 0)
    copy.start()
    copy.wait()
    half[...] += part[core]

    def scatter(d):
        to = (plane + d) % PLANE
        return pltpu.make_async_remote_copy(
            src_ref=half.at[to], dst_ref=slots.at[d],
            send_sem=plane_sem.at[0, 0, d], recv_sem=plane_sem.at[0, 1, d],
            device_id=device(z, to, core), device_id_type=MESH)

    loop(1, PLANE, lambda d: scatter(d).start())
    loop(1, PLANE, lambda d: scatter(d).wait())
    total = half[plane]
    for d in range(1, PLANE):
        total += slots[d]
    zslots[z] = total

    def spread(d):
        return pltpu.make_async_remote_copy(
            src_ref=zslots.at[z], dst_ref=zslots.at[z],
            send_sem=z_sem.at[0, d], recv_sem=z_sem.at[1, d],
            device_id=device((z + d) % NZC, plane, core), device_id_type=MESH)

    loop(1, NZC, lambda d: spread(d).start())
    loop(1, NZC, lambda d: spread(d).wait())
    total = zslots[0]
    for k in range(1, NZC):
        total += zslots[k]
    out[core, plane] = total

    def gather(d):
        return pltpu.make_async_remote_copy(
            src_ref=out.at[core, plane], dst_ref=out.at[core, plane],
            send_sem=plane_sem.at[1, 0, d], recv_sem=plane_sem.at[1, 1, d],
            device_id=device(z, (plane + d) % PLANE, core), device_id_type=MESH)

    def forward(k):
        return core_copy(out.at[core, k], out.at[core, k], 1 + k)

    loop(1, PLANE, lambda d: gather(d).start())
    forward(plane).start()

    def pass_on(d):
        gather(d).wait_recv()
        forward((plane + PLANE - d) % PLANE).start()

    loop(1, PLANE, pass_on)
    loop(1, PLANE, lambda d: gather(d).wait_send())
    loop(0, PLANE, lambda k: forward(k).wait())


PAIRS = [(0, 0), (0, 1), (0, 2), (1, 1), (1, 2), (2, 2)]


def split(a):
    hi = a.astype(BF16)
    rest = a - hi.astype(F32)
    mid = rest.astype(BF16)
    return hi, mid, (rest - mid.astype(F32)).astype(BF16)


def dot(a, b, turned=False):
    dims = (((1,), (1 if turned else 0,)), ((), ()))
    n = a[0].shape[0]

    def term(count, j):
        left = a[0] if count == 1 else jnp.concatenate(a[:count], axis=0)
        out = lax.dot_general(left, b[j], dims, preferred_element_type=F32)
        return [out[n * i:n * i + n] for i in range(count)]

    hh, mh, lh = term(3, 0)
    hm, mm = term(2, 1)
    hl, = term(1, 2)
    return hh + (hm + mh + (hl + lh + mm))


def dot_wide(a, b):
    def wide(x, y, z, w):
        return jnp.dot(jnp.concatenate([x, y], axis=1), jnp.concatenate([z, w], axis=0), preferred_element_type=F32)

    return wide(a[0], a[1], b[0], b[0]) + (wide(a[0], a[1], b[1], b[1]) + wide(a[2], a[0], b[0], b[2]))


def gram_terms(rows):
    high, mid, low = split(rows)

    def term(a, b):
        return lax.dot_general(a, b, (((1,), (1,)), ((), ())), preferred_element_type=F32)

    return term(high, high) + term(mid, mid), term(high, mid) + term(high, low)


def store_blocks(full, part):
    for k, (a, b) in enumerate(PAIRS):
        flat = k * 128
        while flat < k * 128 + 128:
            inside = flat % 24
            size = min(24 - inside, k * 128 + 128 - flat)
            slab = flat // 24
            row = 128 * a + flat - k * 128
            part[slab // PLANE, slab % PLANE, inside:inside + size, :] = full[row:row + size, 128 * b:128 * b + 128]
            flat += size


def inverse_factor(cross, panel=16):
    rank = cross.shape[0]
    rows = lax.broadcasted_iota(jnp.int32, (panel, 128), 0)
    lanes = lax.broadcasted_iota(jnp.int32, (panel, 128), 1)
    here, rest = cross[:panel], cross[panel:]
    outs = []
    for first in range(0, rank, panel):
        end = first + panel
        columns = [jnp.broadcast_to(here[:, first + j:first + j + 1], (panel, 128)) for j in range(panel)]
        inside = (lanes >= first) & (lanes < end)
        solved = jnp.where(inside, (rows + first == lanes).astype(F32), here)
        lower = solved
        inverse = jnp.zeros((panel, 128), F32)
        for k in range(panel):
            pivot = 1.0 / jnp.broadcast_to(columns[k][k:k + 1], (panel, 128))
            ratio = columns[k] * pivot
            others = jnp.where(rows == k, 0.0, ratio)
            below = jnp.where(rows > k, ratio, 0.0)
            inverse = jnp.where(rows == k, pivot, inverse)
            for j in range(k + 1, panel):
                columns[j] = columns[j] - others * columns[j][k:k + 1]
            solved = solved - others * solved[k:k + 1]
            lower = lower - below * lower[k:k + 1]
        outs.append(jnp.where(lanes < end, lower * jnp.sqrt(inverse), 0.0))
        if end == rank:
            break
        solved = solved * inverse
        after = rest[:panel]
        here = jnp.where(inside, 0.0, after)
        for k in range(panel):
            here = here - jnp.broadcast_to(after[:, first + k:first + k + 1], (panel, 128)) * solved[k:k + 1]
        rest = rest[panel:]
        if end + panel == rank:
            continue

        def place(block):
            parts = [block, jnp.zeros((128 - end, 128), BF16)]
            if first:
                parts = [jnp.zeros((first, 128), BF16)] + parts
            return jnp.concatenate(parts, axis=0)

        high, mid, low = (place(t) for t in split(solved))
        a_high, a_mid, a_low = split(rest)

        def wide(a, b, c, d):
            return jnp.dot(
                jnp.concatenate([a, b], axis=1), jnp.concatenate([c, d], axis=0),
                preferred_element_type=F32)

        update = wide(a_high, a_mid, high, high) + (
            wide(a_high, a_mid, mid, mid) + wide(a_high, a_low, low, high))
        column = lax.broadcasted_iota(jnp.int32, update.shape, 1)
        rest = jnp.where((column >= first) & (column < end), 0.0, rest) - update
    return jnp.concatenate(outs, axis=0)


def iterate(packed, start, gram, own):
    blocks = packed[...].reshape(6, 128, 128)
    upper = {pair: blocks[k] for k, pair in enumerate(PAIRS)}
    full = jnp.concatenate([
        jnp.concatenate([upper[(a, b)] if a <= b else upper[(b, a)].T for b in range(3)], axis=1)
        for a in range(3)], axis=0)
    for k, term in enumerate(split(full)):
        gram[k] = term
    own[...] = start[...]

    def step(_):
        image = dot(split(own[...]), [gram[k] for k in range(3)])
        image = jnp.concatenate([image, jnp.zeros((32, 384), F32)], axis=0)
        parts = split(image)
        cross = dot([t[:96] for t in parts], parts, turned=True)
        own[...] = dot_wide(split(inverse_factor(cross)), parts)

    loop(0, ITERS, step)


def own_rows(parts, first, count):
    row = lax.broadcasted_iota(jnp.int32, (count, 384), 0)
    pick = (lax.broadcasted_iota(jnp.int32, (count, 384), 1) == row + first).astype(BF16)
    dims = (((1,), (1,)), ((), ()))
    high, mid, low = (
        lax.dot_general(pick, t, dims, preferred_element_type=F32) for t in parts)
    return high + mid + low


def greet(barrier):
    gx, gy, z, plane, core = position()
    loop(1, GX, lambda d: signal(barrier, ((gx + d) % GX, gy)))
    signal(barrier, device(z, plane, 1 - core))
    loop(1, PLANE, lambda d: signal(barrier, device(z, (plane + d) % PLANE, core)))
    loop(1, NZC, lambda d: signal(barrier, device((z + d) % NZC, plane, core)))
    return GX - 1 + 1 + PLANE - 1 + NZC - 1


def window_kernel(cells_hbm, start_x_hbm, start_y_hbm, own_x, own_y, out, cells, start_x, start_y, send_x, field,
                  send_y, planes, rows, send_c, basis, gram, sem_in, sem_x, sem_y, sem_c, *sums):
    gx, gy, _, _, _ = position()
    sums_x, sums_y = sums[:len(sums) // 2], sums[len(sums) // 2:]

    def fetch(h):
        return pltpu.make_async_copy(cells_hbm.at[pl.ds(4 * h, 4)], cells.at[pl.ds(4 * h, 4)], sem_in.at[h])

    starts = [
        pltpu.make_async_copy(start_x_hbm, start_x, sem_in.at[CHUNKS]),
        pltpu.make_async_copy(start_y_hbm, start_y, sem_in.at[CHUNKS + 1])]
    for h in range(CHUNKS):
        fetch(h).start()
    for start in starts:
        start.start()
    barrier = pltpu.get_barrier_semaphore()
    count = greet(barrier)

    def turn(h, to, target):
        first = pl.multiple_of(to * 64, 64)
        for k in range(2):
            pair = [cells[4 * h + 2 * k + i, pl.ds(first, 64), :] for i in range(2)]
            target[:, 128 * k:128 * k + 128] = jnp.concatenate(pair, axis=0).T

    def copy_x(h, d):
        to = (gx + d) % GX
        return pltpu.make_async_remote_copy(
            src_ref=send_x.at[h, to], dst_ref=field.at[h, gx],
            send_sem=sem_x.at[0, h, d], recv_sem=sem_x.at[1, h, d],
            device_id=(to, gy), device_id_type=MESH)

    for h in range(CHUNKS):
        fetch(h).wait()
        loop(1, GX, lambda d: turn(h, (gx + d) % GX, send_x.at[h, (gx + d) % GX]))
        if h == 0:
            pl.semaphore_wait(barrier, count)
        loop(1, GX, lambda d: copy_x(h, d).start())
    for h in range(CHUNKS):
        turn(h, gx, field.at[h, gx])
    straight, crossed = 0.0, 0.0
    for h in range(CHUNKS):
        loop(1, GX, lambda d: copy_x(h, d).wait_recv())
        terms = gram_terms(field[h].reshape(384, 256))
        straight, crossed = straight + terms[0], crossed + terms[1]
    store_blocks(straight + (crossed + crossed.T), sums_x[0])
    all_sum(*sums_x)
    for h in range(CHUNKS):
        loop(1, GX, lambda d: copy_x(h, d).wait_send())
    for start in starts:
        start.wait()
    iterate(sums_x[1], start_x, gram, basis)
    parts = split(basis[...])
    own_x[...] = own_rows(parts, gx * 48, 48)

    for h in range(CHUNKS):
        reduced = dot(parts, split(field[h].reshape(384, 256)))
        for k in range(GY):
            send_y[k, :, 256 * h:256 * h + 256] = reduced[3 * k:3 * k + 3, :]

    def copy_y(d):
        to = (gy + d) % GY
        return pltpu.make_async_remote_copy(
            src_ref=send_y.at[to], dst_ref=planes.at[gy],
            send_sem=sem_y.at[0, d], recv_sem=sem_y.at[1, d],
            device_id=(gx, to), device_id_type=MESH)

    loop(1, GY, lambda d: copy_y(d).start())
    planes[gy] = send_y[gy]
    loop(1, GY, lambda d: copy_y(d).wait())
    for y in range(12):
        pieces = [planes[:, r, 64 * y:64 * y + 64] for r in range(3)]
        pieces.append(jnp.zeros((GY, 64), F32))
        for k in range(2):
            rows[k, pl.ds(y, GY, stride=12), :] = jnp.concatenate(pieces[2 * k:2 * k + 2], axis=1)
    straight, crossed = gram_terms(jnp.concatenate([rows[0], rows[1]], axis=1))
    store_blocks(straight + (crossed + crossed.T), sums_y[0])
    all_sum(*sums_y)
    iterate(sums_y[1], start_y, gram, basis)
    parts = split(basis[...])
    own_y[...] = own_rows(parts, gy * 12, 12)

    core = dot(parts, split(jnp.concatenate([rows[0], rows[1]], axis=1)))
    for k in range(GY):
        send_c[k] = core[3 * k:3 * k + 3, :192]
    home = gy // 4
    slot = gx * 4 + gy % 4

    def copy_c(k, to):
        return pltpu.make_async_remote_copy(
            src_ref=send_c.at[k], dst_ref=out.at[to],
            send_sem=sem_c.at[0, k], recv_sem=sem_c.at[1, to],
            device_id=(home, k), device_id_type=MESH)

    def go(k):
        mine = (home == gx) & (k == gy)

        @pl.when(jnp.logical_not(mine))
        def _():
            copy_c(k, slot).start()

        @pl.when(mine)
        def _():
            out[slot] = send_c[k]

    def finish(k):
        @pl.when(jnp.logical_not((home == gx) & (k == gy)))
        def _():
            copy_c(k, slot).wait_send()

        @pl.when(jnp.logical_not((home == gx) & (k == slot)))
        def _():
            copy_c(k, k).wait_recv()

    loop(0, GY, go)
    loop(0, GY, finish)


VM = pl.BlockSpec(memory_space=pltpu.VMEM)


def local(snapshot, start_x, start_y):
    cells = jnp.transpose(snapshot, (1, 2, 3, 0)).reshape(12, 512, 48)
    own_x, own_y, pieces = pl.pallas_call(
        window_kernel,
        out_shape=[jax.ShapeDtypeStruct(shape, F32) for shape in ((48, 96), (12, 96), (GY, 3, 192))],
        in_specs=[pl.BlockSpec(memory_space=pltpu.HBM)] * 3,
        out_specs=[VM] * 3,
        scratch_shapes=[
            pltpu.VMEM((12, 512, 48), F32),
            pltpu.VMEM((96, 384), F32),
            pltpu.VMEM((96, 384), F32),
            pltpu.VMEM((CHUNKS, GX, 48, 256), F32),
            pltpu.VMEM((CHUNKS, GX, 48, 256), F32),
            pltpu.VMEM((GY, 3, 768), F32),
            pltpu.VMEM((GY, 3, 768), F32),
            pltpu.VMEM((2, 384, 128), F32),
            pltpu.VMEM((GY, 3, 192), F32),
            pltpu.VMEM((96, 384), F32),
            pltpu.VMEM((3, 384, 384), BF16),
            pltpu.SemaphoreType.DMA((CHUNKS + 2,)),
            pltpu.SemaphoreType.DMA((2, CHUNKS, GX)),
            pltpu.SemaphoreType.DMA((2, GY)),
            pltpu.SemaphoreType.DMA((2, GY)),
        ] + sum_scratch() + sum_scratch(),
        compiler_params=pltpu.CompilerParams(
            collective_id=1, has_side_effects=True, vmem_limit_bytes=62 * 1024 * 1024),
        name="window",
    )(cells, start_x.T, start_y.T)
    pieces = pieces.reshape(8, 4, 3, 3, 4, 16)
    core = jnp.transpose(pieces, (1, 3, 2, 0, 4, 5)).reshape(12, 3, 32, 16)
    return (own_x, own_y, core)


def solution(mesh):
    in_specs = (P("gx", "gy", None, None), P(), P())
    out_specs = (P("gx", None), P("gy", None), P("gx", "gy", None, None))
    return jax.shard_map(local, mesh=mesh, in_specs=in_specs, out_specs=out_specs, check_vma=False)
```

```python
import jax
import jax.numpy as jnp
from jax import lax
from jax.experimental import pallas as pl
from jax.experimental.pallas import tpu as pltpu
from jax.sharding import PartitionSpec as P

ITERS = 4
MESH = pl.DeviceIdType.MESH
F32 = jnp.float32
BF16 = jnp.bfloat16

NXC, NYC, NZC = 4, 4, 8
GX, GY = 8, 32
CHUNKS = 3
PLANE = NXC * NYC


def position():
    gx, gy = lax.axis_index("gx"), lax.axis_index("gy")
    z = (gy // 8) * 2 + gx // 4
    plane = ((gy // 2) % 4) * 4 + gx % 4
    return gx, gy, z, plane, gy % 2


def device(z, plane, core):
    return ((z % 2) * 4 + plane % 4, (z // 2) * 8 + (plane // 4) * 2 + core)


def loop(low, high, body):
    def step(i, carry):
        body(i)
        return carry

    lax.fori_loop(low, high, step, 0)


def signal(sem, where):
    pl.semaphore_signal(sem, inc=1, device_id=where, device_id_type=MESH)


def sum_scratch():
    return [
        pltpu.VMEM((2, PLANE, 24, 128), F32),
        pltpu.VMEM((2, PLANE, 24, 128), F32),
        pltpu.VMEM((PLANE, 24, 128), F32),
        pltpu.VMEM((PLANE, 24, 128), F32),
        pltpu.VMEM((NZC, 24, 128), F32),
        pltpu.SemaphoreType.DMA((4 + PLANE, 2)),
        pltpu.SemaphoreType.DMA((2, 2, PLANE)),
        pltpu.SemaphoreType.DMA((2, NZC)),
    ]


def all_sum(part, out, half, slots, zslots, core_sem, plane_sem, z_sem):
    _, _, z, plane, core = position()

    def core_copy(src, dst, k):
        return pltpu.make_async_remote_copy(
            src_ref=src, dst_ref=dst, send_sem=core_sem.at[k, 0], recv_sem=core_sem.at[k, 1],
            device_id=device(z, plane, 1 - core), device_id_type=MESH)

    def lend(row):
        here = pl.ds(4 * row, 4)
        return core_copy(part.at[1 - core, here], half.at[here], row)

    def scatter(to):
        d = (to + PLANE - plane) % PLANE
        return pltpu.make_async_remote_copy(
            src_ref=half.at[to], dst_ref=slots.at[d],
            send_sem=plane_sem.at[0, 0, d], recv_sem=plane_sem.at[0, 1, d],
            device_id=device(z, to, core), device_id_type=MESH)

    order = [(plane // 4 + e) % 4 for e in (2, 1, 3, 0)]
    for row in order:
        lend(row).start()
    for e, row in enumerate(order):
        lend(row).wait_recv()
        here = pl.ds(4 * row, 4)
        half[here] += part[core, here]
        for i in range(1 if e == 3 else 0, 4):
            scatter(4 * row + (plane + i) % 4).start()
    loop(1, PLANE, lambda d: scatter((plane + d) % PLANE).wait())
    loop(0, 4, lambda row: lend(row).wait_send())
    total = half[plane]
    for d in range(1, PLANE):
        total += slots[d]
    zslots[z] = total

    def spread(d):
        return pltpu.make_async_remote_copy(
            src_ref=zslots.at[z], dst_ref=zslots.at[z],
            send_sem=z_sem.at[0, d], recv_sem=z_sem.at[1, d],
            device_id=device((z + d) % NZC, plane, core), device_id_type=MESH)

    loop(1, NZC, lambda d: spread(d).start())
    loop(1, NZC, lambda d: spread(d).wait())
    total = zslots[0]
    for k in range(1, NZC):
        total += zslots[k]
    out[core, plane] = total

    def gather(d):
        return pltpu.make_async_remote_copy(
            src_ref=out.at[core, plane], dst_ref=out.at[core, plane],
            send_sem=plane_sem.at[1, 0, d], recv_sem=plane_sem.at[1, 1, d],
            device_id=device(z, (plane + d) % PLANE, core), device_id_type=MESH)

    def forward(k):
        return core_copy(out.at[core, k], out.at[core, k], 4 + k)

    loop(1, PLANE, lambda d: gather(d).start())
    forward(plane).start()

    def pass_on(d):
        gather(d).wait_recv()
        forward((plane + PLANE - d) % PLANE).start()

    loop(1, PLANE, pass_on)
    loop(1, PLANE, lambda d: gather(d).wait_send())
    loop(0, PLANE, lambda k: forward(k).wait())


PAIRS = [(0, 0), (0, 1), (0, 2), (1, 1), (1, 2), (2, 2)]


def split(a):
    hi = a.astype(BF16)
    rest = a - hi.astype(F32)
    mid = rest.astype(BF16)
    return hi, mid, (rest - mid.astype(F32)).astype(BF16)


def dot(a, b, turned=False):
    dims = (((1,), (1 if turned else 0,)), ((), ()))
    n = a[0].shape[0]

    def term(count, j):
        left = a[0] if count == 1 else jnp.concatenate(a[:count], axis=0)
        out = lax.dot_general(left, b[j], dims, preferred_element_type=F32)
        return [out[n * i:n * i + n] for i in range(count)]

    hh, mh, lh = term(3, 0)
    hm, mm = term(2, 1)
    hl, = term(1, 2)
    return hh + (hm + mh + (hl + lh + mm))


def dot_wide(a, b):
    def wide(x, y, z, w):
        return jnp.dot(jnp.concatenate([x, y], axis=1), jnp.concatenate([z, w], axis=0), preferred_element_type=F32)

    return wide(a[0], a[1], b[0], b[0]) + (wide(a[0], a[1], b[1], b[1]) + wide(a[2], a[0], b[0], b[2]))


def gram_terms(high, mid, low):
    def term(a, b):
        return lax.dot_general(a, b, (((1,), (1,)), ((), ())), preferred_element_type=F32)

    return term(high, high) + term(mid, mid), term(high, mid) + term(high, low)


def store_blocks(full, part):
    for k, (a, b) in enumerate(PAIRS):
        flat = k * 128
        while flat < k * 128 + 128:
            inside = flat % 24
            size = min(24 - inside, k * 128 + 128 - flat)
            slab = flat // 24
            row = 128 * a + flat - k * 128
            part[slab // PLANE, slab % PLANE, inside:inside + size, :] = full[row:row + size, 128 * b:128 * b + 128]
            flat += size


def inverse_factor(cross, panel=16):
    rank = cross.shape[0]
    rows = lax.broadcasted_iota(jnp.int32, (panel, 128), 0)
    lanes = lax.broadcasted_iota(jnp.int32, (panel, 128), 1)
    here, rest = cross[:panel], cross[panel:]
    outs = []
    for first in range(0, rank, panel):
        end = first + panel
        columns = [jnp.broadcast_to(here[:, first + j:first + j + 1], (panel, 128)) for j in range(panel)]
        inside = (lanes >= first) & (lanes < end)
        solved = jnp.where(inside, (rows + first == lanes).astype(F32), here)
        lower = solved
        inverse = jnp.zeros((panel, 128), F32)
        for k in range(panel):
            pivot = 1.0 / jnp.broadcast_to(columns[k][k:k + 1], (panel, 128))
            ratio = columns[k] * pivot
            others = jnp.where(rows == k, 0.0, ratio)
            below = jnp.where(rows > k, ratio, 0.0)
            inverse = jnp.where(rows == k, pivot, inverse)
            for j in range(k + 1, panel):
                columns[j] = columns[j] - others * columns[j][k:k + 1]
            solved = solved - others * solved[k:k + 1]
            lower = lower - below * lower[k:k + 1]
        outs.append(jnp.where(lanes < end, lower * jnp.sqrt(inverse), 0.0))
        if end == rank:
            break
        solved = solved * inverse
        after = rest[:panel]
        here = jnp.where(inside, 0.0, after)
        for k in range(panel):
            here = here - jnp.broadcast_to(after[:, first + k:first + k + 1], (panel, 128)) * solved[k:k + 1]
        rest = rest[panel:]
        if end + panel == rank:
            continue

        def place(block):
            parts = [block, jnp.zeros((128 - end, 128), BF16)]
            if first:
                parts = [jnp.zeros((first, 128), BF16)] + parts
            return jnp.concatenate(parts, axis=0)

        high, mid, low = (place(t) for t in split(solved))
        a_high, a_mid, a_low = split(rest)

        def wide(a, b, c, d):
            return jnp.dot(
                jnp.concatenate([a, b], axis=1), jnp.concatenate([c, d], axis=0),
                preferred_element_type=F32)

        update = wide(a_high, a_mid, high, high) + (
            wide(a_high, a_mid, mid, mid) + wide(a_high, a_low, low, high))
        column = lax.broadcasted_iota(jnp.int32, update.shape, 1)
        rest = jnp.where((column >= first) & (column < end), 0.0, rest) - update
    return jnp.concatenate(outs, axis=0)


def iterate(packed, start, gram, own):
    blocks = packed[...].reshape(6, 128, 128)
    upper = {pair: blocks[k] for k, pair in enumerate(PAIRS)}
    full = jnp.concatenate([
        jnp.concatenate([upper[(a, b)] if a <= b else upper[(b, a)].T for b in range(3)], axis=1)
        for a in range(3)], axis=0)
    for k, term in enumerate(split(full)):
        gram[k] = term
    own[...] = start[...]

    def step(_):
        image = dot(split(own[...]), [gram[k] for k in range(3)])
        image = jnp.concatenate([image, jnp.zeros((32, 384), F32)], axis=0)
        parts = split(image)
        cross = dot([t[:96] for t in parts], parts, turned=True)
        own[...] = dot_wide(split(inverse_factor(cross)), parts)

    loop(0, ITERS, step)


def own_rows(parts, first, count):
    row = lax.broadcasted_iota(jnp.int32, (count, 384), 0)
    pick = (lax.broadcasted_iota(jnp.int32, (count, 384), 1) == row + first).astype(BF16)
    dims = (((1,), (1,)), ((), ()))
    high, mid, low = (
        lax.dot_general(pick, t, dims, preferred_element_type=F32) for t in parts)
    return high + mid + low


def greet(barrier):
    gx, gy, z, plane, core = position()
    loop(1, GX, lambda d: signal(barrier, ((gx + d) % GX, gy)))
    signal(barrier, device(z, plane, 1 - core))
    loop(1, PLANE, lambda d: signal(barrier, device(z, (plane + d) % PLANE, core)))
    loop(1, NZC, lambda d: signal(barrier, device((z + d) % NZC, plane, core)))
    return GX - 1 + 1 + PLANE - 1 + NZC - 1


def window_kernel(cells_hbm, start_x_hbm, start_y_hbm, own_x, own_y, out, cells, start_x, start_y, send_x, field, field_terms,
                  send_y, planes, rows, send_c, basis, gram, sem_in, sem_x, sem_y, sem_c, *sums):
    gx, gy, _, _, _ = position()
    sums_x, sums_y = sums[:len(sums) // 2], sums[len(sums) // 2:]

    def fetch(h):
        return pltpu.make_async_copy(cells_hbm.at[pl.ds(4 * h, 4)], cells.at[pl.ds(4 * h, 4)], sem_in.at[h])

    starts = [
        pltpu.make_async_copy(start_x_hbm, start_x, sem_in.at[CHUNKS]),
        pltpu.make_async_copy(start_y_hbm, start_y, sem_in.at[CHUNKS + 1])]
    for h in range(CHUNKS):
        fetch(h).start()
    for start in starts:
        start.start()
    barrier = pltpu.get_barrier_semaphore()
    count = greet(barrier)

    def turn(h, to, target):
        for k in range(2):
            slabs = [
                cells[4 * h + 2 * k + i, pl.ds(pl.multiple_of(16 * (8 * z + to), 16), 16), :]
                for i in range(2) for z in range(4)]
            target[:, 128 * k:128 * k + 128] = jnp.concatenate(slabs, axis=0).T

    def copy_x(h, d):
        to = (gx + d) % GX
        return pltpu.make_async_remote_copy(
            src_ref=send_x.at[h, to], dst_ref=field.at[h, gx],
            send_sem=sem_x.at[0, h, d], recv_sem=sem_x.at[1, h, d],
            device_id=(to, gy), device_id_type=MESH)

    for h in range(CHUNKS):
        fetch(h).wait()
        loop(1, GX, lambda d: turn(h, (gx + d) % GX, send_x.at[h, (gx + d) % GX]))
        if h == 0:
            pl.semaphore_wait(barrier, count)
        loop(1, GX, lambda d: copy_x(h, d).start())
    for h in range(CHUNKS):
        turn(h, gx, field.at[h, gx])
    straight, crossed = 0.0, 0.0
    for h in range(CHUNKS):
        loop(1, GX, lambda d: copy_x(h, d).wait_recv())
        terms = split(field[h].reshape(384, 256))
        for k in range(3):
            field_terms[h, k] = terms[k]
        more = gram_terms(*terms)
        straight, crossed = straight + more[0], crossed + more[1]
    store_blocks(straight + (crossed + crossed.T), sums_x[0])
    all_sum(*sums_x)
    for h in range(CHUNKS):
        loop(1, GX, lambda d: copy_x(h, d).wait_send())
    for start in starts:
        start.wait()
    iterate(sums_x[1], start_x, gram, basis)
    parts = split(basis[...])

    for h in range(CHUNKS):
        reduced = dot(parts, [field_terms[h, k] for k in range(3)])
        for k in range(GY):
            send_y[k, :, 256 * h:256 * h + 256] = reduced[3 * k:3 * k + 3, :]

    def copy_y(d):
        to = (gy + d) % GY
        return pltpu.make_async_remote_copy(
            src_ref=send_y.at[to], dst_ref=planes.at[gy],
            send_sem=sem_y.at[0, d], recv_sem=sem_y.at[1, d],
            device_id=(gx, to), device_id_type=MESH)

    loop(1, GY, lambda d: copy_y(d).start())
    planes[gy] = send_y[gy]
    own_x[...] = own_rows(parts, gx * 48, 48)
    loop(1, GY, lambda d: copy_y(d).wait())
    for y in range(12):
        pieces = [planes[:, r, 64 * y:64 * y + 64] for r in range(3)]
        pieces.append(jnp.zeros((GY, 64), F32))
        for k in range(2):
            rows[k, pl.ds(y, GY, stride=12), :] = jnp.concatenate(pieces[2 * k:2 * k + 2], axis=1)
    straight, crossed = gram_terms(*split(jnp.concatenate([rows[0], rows[1]], axis=1)))
    store_blocks(straight + (crossed + crossed.T), sums_y[0])
    all_sum(*sums_y)
    iterate(sums_y[1], start_y, gram, basis)
    parts = split(basis[...])

    core = dot(parts, split(jnp.concatenate([rows[0], rows[1]], axis=1)))
    for k in range(GY):
        send_c[k] = core[3 * k:3 * k + 3, :192]
    home = gy // 4
    slot = gx * 4 + gy % 4

    def copy_c(k, to):
        return pltpu.make_async_remote_copy(
            src_ref=send_c.at[k], dst_ref=out.at[to],
            send_sem=sem_c.at[0, k], recv_sem=sem_c.at[1, to],
            device_id=(home, k), device_id_type=MESH)

    def go(k):
        mine = (home == gx) & (k == gy)

        @pl.when(jnp.logical_not(mine))
        def _():
            copy_c(k, slot).start()

        @pl.when(mine)
        def _():
            out[slot] = send_c[k]

    def finish(k):
        @pl.when(jnp.logical_not((home == gx) & (k == gy)))
        def _():
            copy_c(k, slot).wait_send()

        @pl.when(jnp.logical_not((home == gx) & (k == slot)))
        def _():
            copy_c(k, k).wait_recv()

    loop(0, GY, go)
    own_y[...] = own_rows(parts, gy * 12, 12)
    loop(0, GY, finish)


def results_kernel(own_x, own_y, pieces, basis_x, basis_y, core):
    basis_x[...] = own_x[...]
    basis_y[...] = own_y[...]
    for j in range(4):
        for s in range(3):
            block = jnp.concatenate([pieces[4 * i + j, s:s + 1, :] for i in range(8)], axis=0).T
            for r in range(3):
                quarters = [block[64 * r + 16 * z:64 * r + 16 * z + 16] for z in range(4)]
                core[3 * j + r, s] = jnp.concatenate(quarters, axis=1)


VM = pl.BlockSpec(memory_space=pltpu.VMEM)


def local(snapshot, start_x, start_y):
    cells = jnp.transpose(snapshot, (1, 2, 3, 0)).reshape(12, 512, 48)
    own_x, own_y, pieces = pl.pallas_call(
        window_kernel,
        out_shape=[jax.ShapeDtypeStruct(shape, F32) for shape in ((48, 96), (12, 96), (GY, 3, 192))],
        in_specs=[pl.BlockSpec(memory_space=pltpu.HBM)] * 3,
        out_specs=[VM] * 3,
        scratch_shapes=[
            pltpu.VMEM((12, 512, 48), F32),
            pltpu.VMEM((96, 384), F32),
            pltpu.VMEM((96, 384), F32),
            pltpu.VMEM((CHUNKS, GX, 48, 256), F32),
            pltpu.VMEM((CHUNKS, GX, 48, 256), F32),
            pltpu.VMEM((CHUNKS, 3, 384, 256), BF16),
            pltpu.VMEM((GY, 3, 768), F32),
            pltpu.VMEM((GY, 3, 768), F32),
            pltpu.VMEM((2, 384, 128), F32),
            pltpu.VMEM((GY, 3, 192), F32),
            pltpu.VMEM((96, 384), F32),
            pltpu.VMEM((3, 384, 384), BF16),
            pltpu.SemaphoreType.DMA((CHUNKS + 2,)),
            pltpu.SemaphoreType.DMA((2, CHUNKS, GX)),
            pltpu.SemaphoreType.DMA((2, GY)),
            pltpu.SemaphoreType.DMA((2, GY)),
        ] + sum_scratch() + sum_scratch(),
        compiler_params=pltpu.CompilerParams(
            collective_id=1, has_side_effects=True, vmem_limit_bytes=62 * 1024 * 1024),
        name="window",
    )(cells, start_x.T, start_y.T)
    basis_x, basis_y, core = pl.pallas_call(
        results_kernel,
        out_shape=[jax.ShapeDtypeStruct(shape, F32) for shape in ((48, 96), (12, 96), (12, 3, 16, 32))],
        in_specs=[VM] * 3,
        out_specs=[VM] * 3,
        compiler_params=pltpu.CompilerParams(vmem_limit_bytes=62 * 1024 * 1024),
        name="results",
    )(own_x, own_y, pieces)
    return (basis_x, basis_y, jnp.transpose(core, (0, 1, 3, 2)))


def solution(mesh):
    in_specs = (P("gx", "gy", None, None), P(), P())
    out_specs = (P("gx", None), P("gy", None), P("gx", "gy", None, None))
    return jax.shard_map(local, mesh=mesh, in_specs=in_specs, out_specs=out_specs, check_vma=False)
```

```python
import jax
import jax.numpy as jnp
from jax import lax
from jax.experimental import pallas as pl
from jax.experimental.pallas import tpu as pltpu
from jax.sharding import PartitionSpec as P

ITERS = 4
MESH = pl.DeviceIdType.MESH
F32 = jnp.float32
BF16 = jnp.bfloat16

NXC, NYC, NZC = 4, 4, 8
GX, GY = 8, 32
CHUNKS = 3
PLANE = NXC * NYC
X_STEPS = ((1, 0), (1, 1), (0, 3), (1, 3), (0, 1), (1, 2), (0, 2))
Y_STEPS = (
    21, 20, 22, 23, 18, 19, 28, 13, 29, 17, 16, 12, 10, 15, 11, 14,
    27, 31, 26, 30, 24, 4, 9, 25, 5, 8, 2, 6, 7, 3, 1)
Z_STEPS = (4, 3, 5, 2, 6, 1, 7)
PLANE_STEPS = (10, 6, 14, 9, 11, 2, 8, 5, 7, 13, 15, 1, 3, 4, 12)


def position():
    gx, gy = lax.axis_index("gx"), lax.axis_index("gy")
    z = (gy // 8) * 2 + gx // 4
    plane = ((gy // 2) % 4) * 4 + gx % 4
    return gx, gy, z, plane, gy % 2


def device(z, plane, core):
    return ((z % 2) * 4 + plane % 4, (z // 2) * 8 + (plane // 4) * 2 + core)


def loop(low, high, body):
    def step(i, carry):
        body(i)
        return carry

    lax.fori_loop(low, high, step, 0)


def signal(sem, where):
    pl.semaphore_signal(sem, inc=1, device_id=where, device_id_type=MESH)


def sum_scratch():
    return [
        pltpu.VMEM((2, PLANE, 24, 128), F32),
        pltpu.VMEM((2, PLANE, 24, 128), F32),
        pltpu.VMEM((PLANE, 24, 128), F32),
        pltpu.VMEM((PLANE, 24, 128), F32),
        pltpu.VMEM((NZC, 24, 128), F32),
        pltpu.SemaphoreType.DMA((4 + PLANE, 2)),
        pltpu.SemaphoreType.DMA((2, 2, PLANE)),
        pltpu.SemaphoreType.DMA((2, NZC)),
    ]


def all_sum(part, out, half, slots, zslots, core_sem, plane_sem, z_sem):
    _, _, z, plane, core = position()

    def core_copy(src, dst, k):
        return pltpu.make_async_remote_copy(
            src_ref=src, dst_ref=dst, send_sem=core_sem.at[k, 0], recv_sem=core_sem.at[k, 1],
            device_id=device(z, plane, 1 - core), device_id_type=MESH)

    def lend(row):
        here = pl.ds(4 * row, 4)
        return core_copy(part.at[1 - core, here], half.at[here], row)

    def scatter(to):
        d = (to + PLANE - plane) % PLANE
        return pltpu.make_async_remote_copy(
            src_ref=half.at[to], dst_ref=slots.at[d],
            send_sem=plane_sem.at[0, 0, d], recv_sem=plane_sem.at[0, 1, d],
            device_id=device(z, to, core), device_id_type=MESH)

    order = [(plane // 4 + e) % 4 for e in (2, 1, 3, 0)]
    for row in order:
        lend(row).start()
    for e, row in enumerate(order):
        lend(row).wait_recv()
        here = pl.ds(4 * row, 4)
        half[here] += part[core, here]
        for i in range(1 if e == 3 else 0, 4):
            scatter(4 * row + (plane + i) % 4).start()
    loop(1, PLANE, lambda d: scatter((plane + d) % PLANE).wait())
    loop(0, 4, lambda row: lend(row).wait_send())
    total = half[plane]
    for d in range(1, PLANE):
        total += slots[d]
    zslots[z] = total

    def spread(d):
        return pltpu.make_async_remote_copy(
            src_ref=zslots.at[z], dst_ref=zslots.at[z],
            send_sem=z_sem.at[0, d], recv_sem=z_sem.at[1, d],
            device_id=device((z + d) % NZC, plane, core), device_id_type=MESH)

    for d in Z_STEPS:
        spread(d).start()
    loop(1, NZC, lambda d: spread(d).wait())
    total = zslots[0]
    for k in range(1, NZC):
        total += zslots[k]
    out[core, plane] = total

    def beyond(step):
        return (plane // 4 + step // 4) % 4 * 4 + (plane + step) % 4

    def gather(step):
        return pltpu.make_async_remote_copy(
            src_ref=out.at[core, plane], dst_ref=out.at[core, plane],
            send_sem=plane_sem.at[1, 0, step], recv_sem=plane_sem.at[1, 1, step],
            device_id=device(z, beyond(step), core), device_id_type=MESH)

    def forward(k):
        return core_copy(out.at[core, k], out.at[core, k], 4 + k)

    for step in PLANE_STEPS:
        gather(step).start()
    forward(plane).start()
    for step in PLANE_STEPS[::-1]:
        gather(step).wait_recv()
        forward(beyond((4 - step // 4) % 4 * 4 + (4 - step % 4) % 4)).start()
    loop(1, PLANE, lambda step: gather(step).wait_send())
    loop(0, PLANE, lambda k: forward(k).wait())


PAIRS = [(0, 0), (0, 1), (0, 2), (1, 1), (1, 2), (2, 2)]


def split(a):
    hi = a.astype(BF16)
    rest = a - hi.astype(F32)
    mid = rest.astype(BF16)
    return hi, mid, (rest - mid.astype(F32)).astype(BF16)


def dot(a, b, turned=False):
    dims = (((1,), (1 if turned else 0,)), ((), ()))
    n = a[0].shape[0]

    def term(count, j):
        left = a[0] if count == 1 else jnp.concatenate(a[:count], axis=0)
        out = lax.dot_general(left, b[j], dims, preferred_element_type=F32)
        return [out[n * i:n * i + n] for i in range(count)]

    hh, mh, lh = term(3, 0)
    hm, mm = term(2, 1)
    hl, = term(1, 2)
    return hh + (hm + mh + (hl + lh + mm))


def dot_wide(a, b):
    def wide(x, y, z, w):
        return jnp.dot(jnp.concatenate([x, y], axis=1), jnp.concatenate([z, w], axis=0), preferred_element_type=F32)

    return wide(a[0], a[1], b[0], b[0]) + (wide(a[0], a[1], b[1], b[1]) + wide(a[2], a[0], b[0], b[2]))


def gram_terms(high, mid, low):
    def term(a, b):
        return lax.dot_general(a, b, (((1,), (1,)), ((), ())), preferred_element_type=F32)

    return term(high, high) + term(mid, mid), term(high, mid) + term(high, low)


def store_blocks(full, part):
    for k, (a, b) in enumerate(PAIRS):
        flat = k * 128
        while flat < k * 128 + 128:
            inside = flat % 24
            size = min(24 - inside, k * 128 + 128 - flat)
            slab = flat // 24
            row = 128 * a + flat - k * 128
            part[slab // PLANE, slab % PLANE, inside:inside + size, :] = full[row:row + size, 128 * b:128 * b + 128]
            flat += size


def inverse_factor(cross, panel=16):
    rank = cross.shape[0]
    rows = lax.broadcasted_iota(jnp.int32, (panel, 128), 0)
    lanes = lax.broadcasted_iota(jnp.int32, (panel, 128), 1)
    here, rest = cross[:panel], cross[panel:]
    outs = []
    for first in range(0, rank, panel):
        end = first + panel
        columns = [jnp.broadcast_to(here[:, first + j:first + j + 1], (panel, 128)) for j in range(panel)]
        inside = (lanes >= first) & (lanes < end)
        solved = jnp.where(inside, (rows + first == lanes).astype(F32), here)
        lower = solved
        inverse = jnp.zeros((panel, 128), F32)
        for k in range(panel):
            pivot = 1.0 / jnp.broadcast_to(columns[k][k:k + 1], (panel, 128))
            ratio = columns[k] * pivot
            others = jnp.where(rows == k, 0.0, ratio)
            below = jnp.where(rows > k, ratio, 0.0)
            inverse = jnp.where(rows == k, pivot, inverse)
            for j in range(k + 1, panel):
                columns[j] = columns[j] - others * columns[j][k:k + 1]
            solved = solved - others * solved[k:k + 1]
            lower = lower - below * lower[k:k + 1]
        outs.append(jnp.where(lanes < end, lower * jnp.sqrt(inverse), 0.0))
        if end == rank:
            break
        solved = solved * inverse
        after = rest[:panel]
        here = jnp.where(inside, 0.0, after)
        for k in range(panel):
            here = here - jnp.broadcast_to(after[:, first + k:first + k + 1], (panel, 128)) * solved[k:k + 1]
        rest = rest[panel:]
        if end + panel == rank:
            continue

        def place(block):
            parts = [block, jnp.zeros((128 - end, 128), BF16)]
            if first:
                parts = [jnp.zeros((first, 128), BF16)] + parts
            return jnp.concatenate(parts, axis=0)

        high, mid, low = (place(t) for t in split(solved))
        a_high, a_mid, a_low = split(rest)

        def wide(a, b, c, d):
            return jnp.dot(
                jnp.concatenate([a, b], axis=1), jnp.concatenate([c, d], axis=0),
                preferred_element_type=F32)

        update = wide(a_high, a_mid, high, high) + (
            wide(a_high, a_mid, mid, mid) + wide(a_high, a_low, low, high))
        column = lax.broadcasted_iota(jnp.int32, update.shape, 1)
        rest = jnp.where((column >= first) & (column < end), 0.0, rest) - update
    return jnp.concatenate(outs, axis=0)


def iterate(packed, start, gram, own):
    blocks = packed[...].reshape(6, 128, 128)
    upper = {pair: blocks[k] for k, pair in enumerate(PAIRS)}
    full = jnp.concatenate([
        jnp.concatenate([upper[(a, b)] if a <= b else upper[(b, a)].T for b in range(3)], axis=1)
        for a in range(3)], axis=0)
    for k, term in enumerate(split(full)):
        gram[k] = term
    own[...] = start[...]

    def step(_):
        image = dot(split(own[...]), [gram[k] for k in range(3)])
        image = jnp.concatenate([image, jnp.zeros((32, 384), F32)], axis=0)
        parts = split(image)
        cross = dot([t[:96] for t in parts], parts, turned=True)
        own[...] = dot_wide(split(inverse_factor(cross)), parts)

    loop(0, ITERS, step)


def own_rows(parts, first, count):
    row = lax.broadcasted_iota(jnp.int32, (count, 384), 0)
    pick = (lax.broadcasted_iota(jnp.int32, (count, 384), 1) == row + first).astype(BF16)
    dims = (((1,), (1,)), ((), ()))
    high, mid, low = (
        lax.dot_general(pick, t, dims, preferred_element_type=F32) for t in parts)
    return high + mid + low


def greet(barrier):
    gx, gy, z, plane, core = position()
    loop(1, GX, lambda d: signal(barrier, ((gx + d) % GX, gy)))
    signal(barrier, device(z, plane, 1 - core))
    loop(1, PLANE, lambda d: signal(barrier, device(z, (plane + d) % PLANE, core)))
    loop(1, NZC, lambda d: signal(barrier, device((z + d) % NZC, plane, core)))
    return GX - 1 + 1 + PLANE - 1 + NZC - 1


def window_kernel(cells_hbm, start_x_hbm, start_y_hbm, own_x, own_y, out, cells, start_x, start_y, send_x, field, field_terms,
                  send_y, planes, rows, send_c, basis, gram, sem_in, sem_x, sem_y, sem_c, *sums):
    gx, gy, _, _, _ = position()
    sums_x, sums_y = sums[:len(sums) // 2], sums[len(sums) // 2:]

    def fetch(h):
        return pltpu.make_async_copy(cells_hbm.at[pl.ds(4 * h, 4)], cells.at[pl.ds(4 * h, 4)], sem_in.at[h])

    starts = [
        pltpu.make_async_copy(start_x_hbm, start_x, sem_in.at[CHUNKS]),
        pltpu.make_async_copy(start_y_hbm, start_y, sem_in.at[CHUNKS + 1])]
    for h in range(CHUNKS):
        fetch(h).start()
    for start in starts:
        start.start()
    barrier = pltpu.get_barrier_semaphore()
    count = greet(barrier)

    def turn(h, to, target):
        for k in range(2):
            slabs = [
                cells[4 * h + 2 * k + i, pl.ds(pl.multiple_of(16 * (8 * z + to), 16), 16), :]
                for i in range(2) for z in range(4)]
            target[:, 128 * k:128 * k + 128] = jnp.concatenate(slabs, axis=0).T

    def copy_x(h, d):
        to = (gx // 4 + X_STEPS[d][0]) % 2 * 4 + (gx + X_STEPS[d][1]) % 4
        return pltpu.make_async_remote_copy(
            src_ref=send_x.at[h, to], dst_ref=field.at[h, gx],
            send_sem=sem_x.at[0, h, d], recv_sem=sem_x.at[1, h, d],
            device_id=(to, gy), device_id_type=MESH)

    for h in range(CHUNKS):
        fetch(h).wait()
        loop(1, GX, lambda d: turn(h, (gx + d) % GX, send_x.at[h, (gx + d) % GX]))
        if h == 0:
            pl.semaphore_wait(barrier, count)
        for d in range(GX - 1):
            copy_x(h, d).start()
    for h in range(CHUNKS):
        turn(h, gx, field.at[h, gx])
    straight, crossed = 0.0, 0.0
    for h in range(CHUNKS):
        for d in range(GX - 1):
            copy_x(h, d).wait_recv()
        terms = split(field[h].reshape(384, 256))
        for k in range(3):
            field_terms[h, k] = terms[k]
        more = gram_terms(*terms)
        straight, crossed = straight + more[0], crossed + more[1]
    store_blocks(straight + (crossed + crossed.T), sums_x[0])
    all_sum(*sums_x)
    for h in range(CHUNKS):
        for d in range(GX - 1):
            copy_x(h, d).wait_send()
    for start in starts:
        start.wait()
    iterate(sums_x[1], start_x, gram, basis)
    parts = split(basis[...])

    for h in range(CHUNKS):
        reduced = dot(parts, [field_terms[h, k] for k in range(3)])
        for k in range(GY):
            send_y[k, :, 256 * h:256 * h + 256] = reduced[3 * k:3 * k + 3, :]

    def copy_y(d):
        step = Y_STEPS[d]
        to = (gy // 8 + step // 8) % 4 * 8 + (gy // 2 + step // 2) % 4 * 2 + (gy + step) % 2
        return pltpu.make_async_remote_copy(
            src_ref=send_y.at[to], dst_ref=planes.at[gy],
            send_sem=sem_y.at[0, d], recv_sem=sem_y.at[1, d],
            device_id=(gx, to), device_id_type=MESH)

    for d in range(GY - 1):
        copy_y(d).start()
    planes[gy] = send_y[gy]
    own_x[...] = own_rows(parts, gx * 48, 48)
    for d in range(GY - 1):
        copy_y(d).wait()
    for y in range(12):
        pieces = [planes[:, r, 64 * y:64 * y + 64] for r in range(3)]
        pieces.append(jnp.zeros((GY, 64), F32))
        for k in range(2):
            rows[k, pl.ds(y, GY, stride=12), :] = jnp.concatenate(pieces[2 * k:2 * k + 2], axis=1)
    straight, crossed = gram_terms(*split(jnp.concatenate([rows[0], rows[1]], axis=1)))
    store_blocks(straight + (crossed + crossed.T), sums_y[0])
    all_sum(*sums_y)
    iterate(sums_y[1], start_y, gram, basis)
    parts = split(basis[...])

    core = dot(parts, split(jnp.concatenate([rows[0], rows[1]], axis=1)))
    for k in range(GY):
        send_c[k] = core[3 * k:3 * k + 3, :192]
    home = gy // 4
    slot = gx * 4 + gy % 4

    def copy_c(k, to):
        return pltpu.make_async_remote_copy(
            src_ref=send_c.at[k], dst_ref=out.at[to],
            send_sem=sem_c.at[0, k], recv_sem=sem_c.at[1, to],
            device_id=(home, k), device_id_type=MESH)

    def go(k):
        mine = (home == gx) & (k == gy)

        @pl.when(jnp.logical_not(mine))
        def _():
            copy_c(k, slot).start()

        @pl.when(mine)
        def _():
            out[slot] = send_c[k]

    def finish(k):
        @pl.when(jnp.logical_not((home == gx) & (k == gy)))
        def _():
            copy_c(k, slot).wait_send()

        @pl.when(jnp.logical_not((home == gx) & (k == slot)))
        def _():
            copy_c(k, k).wait_recv()

    loop(0, GY, go)
    own_y[...] = own_rows(parts, gy * 12, 12)
    loop(0, GY, finish)


def results_kernel(own_x, own_y, pieces, basis_x, basis_y, core):
    basis_x[...] = own_x[...]
    basis_y[...] = own_y[...]
    for j in range(4):
        for s in range(3):
            block = jnp.concatenate([pieces[4 * i + j, s:s + 1, :] for i in range(8)], axis=0).T
            for r in range(3):
                quarters = [block[64 * r + 16 * z:64 * r + 16 * z + 16] for z in range(4)]
                core[3 * j + r, s] = jnp.concatenate(quarters, axis=1)


VM = pl.BlockSpec(memory_space=pltpu.VMEM)


def local(snapshot, start_x, start_y):
    cells = jnp.transpose(snapshot, (1, 2, 3, 0)).reshape(12, 512, 48)
    own_x, own_y, pieces = pl.pallas_call(
        window_kernel,
        out_shape=[jax.ShapeDtypeStruct(shape, F32) for shape in ((48, 96), (12, 96), (GY, 3, 192))],
        in_specs=[pl.BlockSpec(memory_space=pltpu.HBM)] * 3,
        out_specs=[VM] * 3,
        scratch_shapes=[
            pltpu.VMEM((12, 512, 48), F32),
            pltpu.VMEM((96, 384), F32),
            pltpu.VMEM((96, 384), F32),
            pltpu.VMEM((CHUNKS, GX, 48, 256), F32),
            pltpu.VMEM((CHUNKS, GX, 48, 256), F32),
            pltpu.VMEM((CHUNKS, 3, 384, 256), BF16),
            pltpu.VMEM((GY, 3, 768), F32),
            pltpu.VMEM((GY, 3, 768), F32),
            pltpu.VMEM((2, 384, 128), F32),
            pltpu.VMEM((GY, 3, 192), F32),
            pltpu.VMEM((96, 384), F32),
            pltpu.VMEM((3, 384, 384), BF16),
            pltpu.SemaphoreType.DMA((CHUNKS + 2,)),
            pltpu.SemaphoreType.DMA((2, CHUNKS, GX)),
            pltpu.SemaphoreType.DMA((2, GY)),
            pltpu.SemaphoreType.DMA((2, GY)),
        ] + sum_scratch() + sum_scratch(),
        compiler_params=pltpu.CompilerParams(
            collective_id=1, has_side_effects=True, vmem_limit_bytes=62 * 1024 * 1024),
        name="window",
    )(cells, start_x.T, start_y.T)
    basis_x, basis_y, core = pl.pallas_call(
        results_kernel,
        out_shape=[jax.ShapeDtypeStruct(shape, F32) for shape in ((48, 96), (12, 96), (12, 3, 16, 32))],
        in_specs=[VM] * 3,
        out_specs=[VM] * 3,
        compiler_params=pltpu.CompilerParams(vmem_limit_bytes=62 * 1024 * 1024),
        name="results",
    )(own_x, own_y, pieces)
    return (basis_x, basis_y, jnp.transpose(core, (0, 1, 3, 2)))


def solution(mesh):
    in_specs = (P("gx", "gy", None, None), P(), P())
    out_specs = (P("gx", None), P("gy", None), P("gx", "gy", None, None))
    return jax.shard_map(local, mesh=mesh, in_specs=in_specs, out_specs=out_specs, check_vma=False)
```

```python
import jax
import jax.numpy as jnp
from jax import lax
from jax.experimental import pallas as pl
from jax.experimental.pallas import tpu as pltpu
from jax.sharding import PartitionSpec as P

ITERS = 4
MESH = pl.DeviceIdType.MESH
F32 = jnp.float32
BF16 = jnp.bfloat16

NXC, NYC, NZC = 4, 4, 8
GX, GY = 8, 32
CHUNKS = 3
PLANE = NXC * NYC
X_STEPS = ((1, 0), (1, 1), (0, 3), (1, 3), (0, 1), (1, 2), (0, 2))
Y_STEPS = (
    21, 20, 22, 23, 18, 19, 28, 13, 29, 17, 16, 12, 10, 15, 11, 14,
    27, 31, 26, 30, 24, 4, 9, 25, 5, 8, 2, 6, 7, 3, 1)
Z_STEPS = (4, 3, 5, 2, 6, 1, 7)
PLANE_STEPS = (10, 6, 14, 9, 11, 2, 8, 5, 7, 13, 15, 1, 3, 4, 12)


def position():
    gx, gy = lax.axis_index("gx"), lax.axis_index("gy")
    z = (gy // 8) * 2 + gx // 4
    plane = ((gy // 2) % 4) * 4 + gx % 4
    return gx, gy, z, plane, gy % 2


def device(z, plane, core):
    return ((z % 2) * 4 + plane % 4, (z // 2) * 8 + (plane // 4) * 2 + core)


def loop(low, high, body):
    def step(i, carry):
        body(i)
        return carry

    lax.fori_loop(low, high, step, 0)


def signal(sem, where):
    pl.semaphore_signal(sem, inc=1, device_id=where, device_id_type=MESH)


def sum_scratch():
    return [
        pltpu.VMEM((2, PLANE, 24, 128), F32),
        pltpu.VMEM((2, PLANE, 24, 128), F32),
        pltpu.VMEM((PLANE, 24, 128), F32),
        pltpu.VMEM((PLANE, 24, 128), F32),
        pltpu.VMEM((NZC, 24, 128), F32),
        pltpu.SemaphoreType.DMA((4 + PLANE, 2)),
        pltpu.SemaphoreType.DMA((2, 2, PLANE)),
        pltpu.SemaphoreType.DMA((2, NZC)),
    ]


def all_sum(part, out, half, slots, zslots, core_sem, plane_sem, z_sem):
    _, _, z, plane, core = position()

    def core_copy(src, dst, k):
        return pltpu.make_async_remote_copy(
            src_ref=src, dst_ref=dst, send_sem=core_sem.at[k, 0], recv_sem=core_sem.at[k, 1],
            device_id=device(z, plane, 1 - core), device_id_type=MESH)

    def lend(row):
        here = pl.ds(4 * row, 4)
        return core_copy(part.at[1 - core, here], half.at[here], row)

    def scatter(to):
        d = (to + PLANE - plane) % PLANE
        return pltpu.make_async_remote_copy(
            src_ref=half.at[to], dst_ref=slots.at[d],
            send_sem=plane_sem.at[0, 0, d], recv_sem=plane_sem.at[0, 1, d],
            device_id=device(z, to, core), device_id_type=MESH)

    order = [(plane // 4 + e) % 4 for e in (2, 1, 3, 0)]
    for row in order:
        lend(row).start()
    for e, row in enumerate(order):
        lend(row).wait_recv()
        here = pl.ds(4 * row, 4)
        half[here] += part[core, here]
        for i in range(1 if e == 3 else 0, 4):
            scatter(4 * row + (plane + i) % 4).start()
    loop(1, PLANE, lambda d: scatter((plane + d) % PLANE).wait())
    loop(0, 4, lambda row: lend(row).wait_send())
    total = half[plane]
    for d in range(1, PLANE):
        total += slots[d]
    zslots[z] = total

    def spread(d):
        return pltpu.make_async_remote_copy(
            src_ref=zslots.at[z], dst_ref=zslots.at[z],
            send_sem=z_sem.at[0, d], recv_sem=z_sem.at[1, d],
            device_id=device((z + d) % NZC, plane, core), device_id_type=MESH)

    for d in Z_STEPS:
        spread(d).start()
    loop(1, NZC, lambda d: spread(d).wait())
    total = zslots[0]
    for k in range(1, NZC):
        total += zslots[k]
    out[core, plane] = total

    def beyond(step):
        return (plane // 4 + step // 4) % 4 * 4 + (plane + step) % 4

    def gather(step):
        return pltpu.make_async_remote_copy(
            src_ref=out.at[core, plane], dst_ref=out.at[core, plane],
            send_sem=plane_sem.at[1, 0, step], recv_sem=plane_sem.at[1, 1, step],
            device_id=device(z, beyond(step), core), device_id_type=MESH)

    def forward(k):
        return core_copy(out.at[core, k], out.at[core, k], 4 + k)

    for step in PLANE_STEPS:
        gather(step).start()
    forward(plane).start()
    for step in PLANE_STEPS[::-1]:
        gather(step).wait_recv()
        forward(beyond((4 - step // 4) % 4 * 4 + (4 - step % 4) % 4)).start()
    loop(1, PLANE, lambda step: gather(step).wait_send())
    loop(0, PLANE, lambda k: forward(k).wait())


PAIRS = [(0, 0), (0, 1), (0, 2), (1, 1), (1, 2), (2, 2)]


def split(a):
    hi = a.astype(BF16)
    rest = a - hi.astype(F32)
    mid = rest.astype(BF16)
    return hi, mid, (rest - mid.astype(F32)).astype(BF16)


def dot(a, b, turned=False):
    dims = (((1,), (1 if turned else 0,)), ((), ()))
    n = a[0].shape[0]

    def term(count, j):
        left = a[0] if count == 1 else jnp.concatenate(a[:count], axis=0)
        out = lax.dot_general(left, b[j], dims, preferred_element_type=F32)
        return [out[n * i:n * i + n] for i in range(count)]

    hh, mh, lh = term(3, 0)
    hm, mm = term(2, 1)
    hl, = term(1, 2)
    return hh + (hm + mh + (hl + lh + mm))


def dot_wide(a, b):
    def wide(x, y, z, w):
        return jnp.dot(jnp.concatenate([x, y], axis=1), jnp.concatenate([z, w], axis=0), preferred_element_type=F32)

    return wide(a[0], a[1], b[0], b[0]) + (wide(a[0], a[1], b[1], b[1]) + wide(a[2], a[0], b[0], b[2]))


def gram_terms(high, mid, low):
    def term(a, b):
        return lax.dot_general(a, b, (((1,), (1,)), ((), ())), preferred_element_type=F32)

    return term(high, high) + term(mid, mid), term(high, mid) + term(high, low)


def store_gram(straight, crossed, part):
    for k, (a, b) in enumerate(PAIRS):
        rows, columns = slice(128 * a, 128 * a + 128), slice(128 * b, 128 * b + 128)
        block = straight[rows, columns] + (crossed[rows, columns] + crossed[columns, rows].T)
        flat = k * 128
        while flat < k * 128 + 128:
            inside = flat % 24
            size = min(24 - inside, k * 128 + 128 - flat)
            slab = flat // 24
            row = flat - k * 128
            part[slab // PLANE, slab % PLANE, inside:inside + size, :] = block[row:row + size]
            flat += size


def inverse_factor(cross, panel=16):
    rank = cross.shape[0]
    rows = lax.broadcasted_iota(jnp.int32, (panel, 128), 0)
    lanes = lax.broadcasted_iota(jnp.int32, (panel, 128), 1)
    here, rest = cross[:panel], cross[panel:]
    outs = []
    for first in range(0, rank, panel):
        end = first + panel
        columns = [jnp.broadcast_to(here[:, first + j:first + j + 1], (panel, 128)) for j in range(panel)]
        inside = (lanes >= first) & (lanes < end)
        solved = jnp.where(inside, (rows + first == lanes).astype(F32), here)
        lower = solved
        inverse = jnp.zeros((panel, 128), F32)
        for k in range(panel):
            pivot = 1.0 / jnp.broadcast_to(columns[k][k:k + 1], (panel, 128))
            ratio = columns[k] * pivot
            others = jnp.where(rows == k, 0.0, ratio)
            below = jnp.where(rows > k, ratio, 0.0)
            inverse = jnp.where(rows == k, pivot, inverse)
            for j in range(k + 1, panel):
                columns[j] = columns[j] - others * columns[j][k:k + 1]
            solved = solved - others * solved[k:k + 1]
            lower = lower - below * lower[k:k + 1]
        outs.append(jnp.where(lanes < end, lower * jnp.sqrt(inverse), 0.0))
        if end == rank:
            break
        solved = solved * inverse
        after = rest[:panel]
        here = jnp.where(inside, 0.0, after)
        for k in range(panel):
            here = here - jnp.broadcast_to(after[:, first + k:first + k + 1], (panel, 128)) * solved[k:k + 1]
        rest = rest[panel:]
        if end + panel == rank:
            continue

        def place(block):
            parts = [block, jnp.zeros((128 - end, 128), BF16)]
            if first:
                parts = [jnp.zeros((first, 128), BF16)] + parts
            return jnp.concatenate(parts, axis=0)

        high, mid, low = (place(t) for t in split(solved))
        a_high, a_mid, a_low = split(rest)

        def wide(a, b, c, d):
            return jnp.dot(
                jnp.concatenate([a, b], axis=1), jnp.concatenate([c, d], axis=0),
                preferred_element_type=F32)

        update = wide(a_high, a_mid, high, high) + (
            wide(a_high, a_mid, mid, mid) + wide(a_high, a_low, low, high))
        column = lax.broadcasted_iota(jnp.int32, update.shape, 1)
        rest = jnp.where((column >= first) & (column < end), 0.0, rest) - update
    return jnp.concatenate(outs, axis=0)


def iterate(packed, start, gram, own):
    blocks = packed[...].reshape(6, 128, 128)
    upper = {pair: blocks[k] for k, pair in enumerate(PAIRS)}
    full = jnp.concatenate([
        jnp.concatenate([upper[(a, b)] if a <= b else upper[(b, a)].T for b in range(3)], axis=1)
        for a in range(3)], axis=0)
    for k, term in enumerate(split(full)):
        gram[k] = term
    own[...] = start[...]

    def step(_):
        parts, cross = image_of(gram, own)
        own[...] = dot_wide(split(inverse_factor(cross)), parts)

    loop(0, ITERS - 1, step)


def image_of(gram, own):
    image = dot(split(own[...]), [gram[k] for k in range(3)])
    parts = split(jnp.concatenate([image, jnp.zeros((32, 384), F32)], axis=0))
    return parts, dot([t[:96] for t in parts], parts, turned=True)


def last_step(gram, own, others):
    parts, cross = image_of(gram, own)
    moved = [split(dot(parts, other)) for other in others]
    inverse = split(inverse_factor(cross))
    return [dot_wide(inverse, m) for m in moved], lambda: split(dot_wide(inverse, parts))


def own_rows(parts, first, count):
    row = lax.broadcasted_iota(jnp.int32, (count, 384), 0)
    pick = (lax.broadcasted_iota(jnp.int32, (count, 384), 1) == row + first).astype(BF16)
    dims = (((1,), (1,)), ((), ()))
    high, mid, low = (
        lax.dot_general(pick, t, dims, preferred_element_type=F32) for t in parts)
    return high + mid + low


def greet(barrier):
    gx, gy, z, plane, core = position()
    loop(1, GX, lambda d: signal(barrier, ((gx + d) % GX, gy)))
    signal(barrier, device(z, plane, 1 - core))
    loop(1, PLANE, lambda d: signal(barrier, device(z, (plane + d) % PLANE, core)))
    loop(1, NZC, lambda d: signal(barrier, device((z + d) % NZC, plane, core)))
    return GX - 1 + 1 + PLANE - 1 + NZC - 1


def window_kernel(cells_hbm, start_x_hbm, start_y_hbm, own_x, own_y, out, cells, start_x, start_y, send_x, field, field_terms,
                  send_y, planes, rows, send_c, basis, gram, sem_in, sem_x, sem_y, sem_c, *sums):
    gx, gy, _, _, _ = position()
    sums_x, sums_y = sums[:len(sums) // 2], sums[len(sums) // 2:]

    barrier = pltpu.get_barrier_semaphore()
    count = greet(barrier)

    def fetch(h):
        return pltpu.make_async_copy(cells_hbm.at[pl.ds(4 * h, 4)], cells.at[pl.ds(4 * h, 4)], sem_in.at[h])

    starts = [
        pltpu.make_async_copy(start_x_hbm, start_x, sem_in.at[CHUNKS]),
        pltpu.make_async_copy(start_y_hbm, start_y, sem_in.at[CHUNKS + 1])]
    for h in range(CHUNKS):
        fetch(h).start()
    for start in starts:
        start.start()

    def turn(h, to, target):
        for k in range(2):
            slabs = [
                cells[4 * h + 2 * k + i, pl.ds(pl.multiple_of(16 * (8 * z + to), 16), 16), :]
                for i in range(2) for z in range(4)]
            target[:, 128 * k:128 * k + 128] = jnp.concatenate(slabs, axis=0).T

    def copy_x(h, d):
        to = (gx // 4 + X_STEPS[d][0]) % 2 * 4 + (gx + X_STEPS[d][1]) % 4
        return pltpu.make_async_remote_copy(
            src_ref=send_x.at[h, to], dst_ref=field.at[h, gx],
            send_sem=sem_x.at[0, h, d], recv_sem=sem_x.at[1, h, d],
            device_id=(to, gy), device_id_type=MESH)

    for h in range(CHUNKS):
        fetch(h).wait()
        loop(1, GX, lambda d: turn(h, (gx + d) % GX, send_x.at[h, (gx + d) % GX]))
        if h == 0:
            pl.semaphore_wait(barrier, count)
        for d in range(GX - 1):
            copy_x(h, d).start()
    for h in range(CHUNKS):
        turn(h, gx, field.at[h, gx])
    straight, crossed = 0.0, 0.0
    for h in range(CHUNKS):
        for d in range(GX - 1):
            copy_x(h, d).wait_recv()
        terms = split(field[h].reshape(384, 256))
        for k in range(3):
            field_terms[h, k] = terms[k]
        more = gram_terms(*terms)
        straight, crossed = straight + more[0], crossed + more[1]
    store_gram(straight, crossed, sums_x[0])
    all_sum(*sums_x)
    for h in range(CHUNKS):
        for d in range(GX - 1):
            copy_x(h, d).wait_send()
    for start in starts:
        start.wait()
    iterate(sums_x[1], start_x, gram, basis)

    reduced_all, terms_x = last_step(
        gram, basis, [[field_terms[h, k] for k in range(3)] for h in range(CHUNKS)])
    for h, reduced in enumerate(reduced_all):
        for k in range(GY):
            send_y[k, :, 256 * h:256 * h + 256] = reduced[3 * k:3 * k + 3, :]

    def copy_y(d):
        step = Y_STEPS[d]
        to = (gy // 8 + step // 8) % 4 * 8 + (gy // 2 + step // 2) % 4 * 2 + (gy + step) % 2
        return pltpu.make_async_remote_copy(
            src_ref=send_y.at[to], dst_ref=planes.at[gy],
            send_sem=sem_y.at[0, d], recv_sem=sem_y.at[1, d],
            device_id=(gx, to), device_id_type=MESH)

    for d in range(GY - 1):
        copy_y(d).start()
    planes[gy] = send_y[gy]
    own_x[...] = own_rows(terms_x(), gx * 48, 48)
    for d in range(GY - 1):
        copy_y(d).wait()
    for y in range(12):
        pieces = [planes[:, r, 64 * y:64 * y + 64] for r in range(3)]
        pieces.append(jnp.zeros((GY, 64), F32))
        for k in range(2):
            rows[k, pl.ds(y, GY, stride=12), :] = jnp.concatenate(pieces[2 * k:2 * k + 2], axis=1)
    straight, crossed = gram_terms(*split(jnp.concatenate([rows[0], rows[1]], axis=1)))
    store_gram(straight, crossed, sums_y[0])
    all_sum(*sums_y)
    iterate(sums_y[1], start_y, gram, basis)

    (core,), terms_y = last_step(gram, basis, [split(jnp.concatenate([rows[0], rows[1]], axis=1))])
    for k in range(GY):
        send_c[k] = core[3 * k:3 * k + 3, :192]
    home = gy // 4
    slot = gx * 4 + gy % 4

    def copy_c(k, to):
        return pltpu.make_async_remote_copy(
            src_ref=send_c.at[k], dst_ref=out.at[to],
            send_sem=sem_c.at[0, k], recv_sem=sem_c.at[1, to],
            device_id=(home, k), device_id_type=MESH)

    def go(k):
        mine = (home == gx) & (k == gy)

        @pl.when(jnp.logical_not(mine))
        def _():
            copy_c(k, slot).start()

        @pl.when(mine)
        def _():
            out[slot] = send_c[k]

    def finish(k):
        @pl.when(jnp.logical_not((home == gx) & (k == gy)))
        def _():
            copy_c(k, slot).wait_send()

        @pl.when(jnp.logical_not((home == gx) & (k == slot)))
        def _():
            copy_c(k, k).wait_recv()

    loop(0, GY, go)
    own_y[...] = own_rows(terms_y(), gy * 12, 12)
    loop(0, GY, finish)


def results_kernel(own_x, own_y, pieces, basis_x, basis_y, core):
    basis_x[...] = own_x[...]
    basis_y[...] = own_y[...]
    for j in range(4):
        for s in range(3):
            block = jnp.concatenate([pieces[4 * i + j, s:s + 1, :] for i in range(8)], axis=0).T
            for r in range(3):
                quarters = [block[64 * r + 16 * z:64 * r + 16 * z + 16] for z in range(4)]
                core[3 * j + r, s] = jnp.concatenate(quarters, axis=1)


VM = pl.BlockSpec(memory_space=pltpu.VMEM)


def local(snapshot, start_x, start_y):
    cells = jnp.transpose(snapshot, (1, 2, 3, 0)).reshape(12, 512, 48)
    own_x, own_y, pieces = pl.pallas_call(
        window_kernel,
        out_shape=[jax.ShapeDtypeStruct(shape, F32) for shape in ((48, 96), (12, 96), (GY, 3, 192))],
        in_specs=[pl.BlockSpec(memory_space=pltpu.HBM)] * 3,
        out_specs=[VM] * 3,
        scratch_shapes=[
            pltpu.VMEM((12, 512, 48), F32),
            pltpu.VMEM((96, 384), F32),
            pltpu.VMEM((96, 384), F32),
            pltpu.VMEM((CHUNKS, GX, 48, 256), F32),
            pltpu.VMEM((CHUNKS, GX, 48, 256), F32),
            pltpu.VMEM((CHUNKS, 3, 384, 256), BF16),
            pltpu.VMEM((GY, 3, 768), F32),
            pltpu.VMEM((GY, 3, 768), F32),
            pltpu.VMEM((2, 384, 128), F32),
            pltpu.VMEM((GY, 3, 192), F32),
            pltpu.VMEM((96, 384), F32),
            pltpu.VMEM((3, 384, 384), BF16),
            pltpu.SemaphoreType.DMA((CHUNKS + 2,)),
            pltpu.SemaphoreType.DMA((2, CHUNKS, GX)),
            pltpu.SemaphoreType.DMA((2, GY)),
            pltpu.SemaphoreType.DMA((2, GY)),
        ] + sum_scratch() + sum_scratch(),
        compiler_params=pltpu.CompilerParams(
            collective_id=1, has_side_effects=True, vmem_limit_bytes=62 * 1024 * 1024),
        name="window",
    )(cells, start_x.T, start_y.T)
    basis_x, basis_y, core = pl.pallas_call(
        results_kernel,
        out_shape=[jax.ShapeDtypeStruct(shape, F32) for shape in ((48, 96), (12, 96), (12, 3, 16, 32))],
        in_specs=[VM] * 3,
        out_specs=[VM] * 3,
        compiler_params=pltpu.CompilerParams(vmem_limit_bytes=62 * 1024 * 1024),
        name="results",
    )(own_x, own_y, pieces)
    return (basis_x, basis_y, jnp.transpose(core, (0, 1, 3, 2)))


def solution(mesh):
    in_specs = (P("gx", "gy", None, None), P(), P())
    out_specs = (P("gx", None), P("gy", None), P("gx", "gy", None, None))
    return jax.shard_map(local, mesh=mesh, in_specs=in_specs, out_specs=out_specs, check_vma=False)
```

```python
import jax
import jax.numpy as jnp
from jax import lax
from jax.experimental import pallas as pl
from jax.experimental.pallas import tpu as pltpu
from jax.sharding import PartitionSpec as P

ITERS = 4
MESH = pl.DeviceIdType.MESH
F32 = jnp.float32
BF16 = jnp.bfloat16

NXC, NYC, NZC = 4, 4, 8
GX, GY = 8, 32
CHUNKS = 3
PLANE = NXC * NYC
X_STEPS = ((1, 0), (1, 1), (0, 3), (1, 3), (0, 1), (1, 2), (0, 2))
Y_STEPS = (
    21, 20, 22, 23, 18, 19, 28, 13, 29, 17, 16, 12, 10, 15, 11, 14,
    27, 31, 26, 30, 24, 4, 9, 25, 5, 8, 2, 6, 7, 3, 1)
Z_STEPS = (4, 3, 5, 2, 6, 1, 7)
PLANE_STEPS = (10, 6, 14, 9, 11, 2, 8, 5, 7, 13, 15, 1, 3, 4, 12)


def position():
    gx, gy = lax.axis_index("gx"), lax.axis_index("gy")
    z = (gy // 8) * 2 + gx // 4
    plane = ((gy // 2) % 4) * 4 + gx % 4
    return gx, gy, z, plane, gy % 2


def device(z, plane, core):
    return ((z % 2) * 4 + plane % 4, (z // 2) * 8 + (plane // 4) * 2 + core)


def loop(low, high, body):
    def step(i, carry):
        body(i)
        return carry

    lax.fori_loop(low, high, step, 0)


def signal(sem, where):
    pl.semaphore_signal(sem, inc=1, device_id=where, device_id_type=MESH)


def sum_scratch():
    return [
        pltpu.VMEM((2, PLANE, 24, 128), F32),
        pltpu.VMEM((2, PLANE, 24, 128), F32),
        pltpu.VMEM((PLANE, 24, 128), F32),
        pltpu.VMEM((PLANE, 24, 128), F32),
        pltpu.VMEM((NZC, 24, 128), F32),
        pltpu.SemaphoreType.DMA((4 + PLANE, 2)),
        pltpu.SemaphoreType.DMA((2, 2, PLANE)),
        pltpu.SemaphoreType.DMA((2, NZC)),
    ]


def all_sum(part, out, half, slots, zslots, core_sem, plane_sem, z_sem):
    _, _, z, plane, core = position()

    def core_copy(src, dst, k):
        return pltpu.make_async_remote_copy(
            src_ref=src, dst_ref=dst, send_sem=core_sem.at[k, 0], recv_sem=core_sem.at[k, 1],
            device_id=device(z, plane, 1 - core), device_id_type=MESH)

    def lend(row):
        here = pl.ds(4 * row, 4)
        return core_copy(part.at[1 - core, here], half.at[here], row)

    def scatter(to):
        d = (to + PLANE - plane) % PLANE
        return pltpu.make_async_remote_copy(
            src_ref=half.at[to], dst_ref=slots.at[d],
            send_sem=plane_sem.at[0, 0, d], recv_sem=plane_sem.at[0, 1, d],
            device_id=device(z, to, core), device_id_type=MESH)

    order = [(plane // 4 + e) % 4 for e in (2, 1, 3, 0)]
    for row in order:
        lend(row).start()
    for e, row in enumerate(order):
        lend(row).wait_recv()
        here = pl.ds(4 * row, 4)
        half[here] += part[core, here]
        for i in range(1 if e == 3 else 0, 4):
            scatter(4 * row + (plane + i) % 4).start()
    loop(1, PLANE, lambda d: scatter((plane + d) % PLANE).wait())
    loop(0, 4, lambda row: lend(row).wait_send())
    total = half[plane]
    for d in range(1, PLANE):
        total += slots[d]
    zslots[z] = total

    def spread(d):
        return pltpu.make_async_remote_copy(
            src_ref=zslots.at[z], dst_ref=zslots.at[z],
            send_sem=z_sem.at[0, d], recv_sem=z_sem.at[1, d],
            device_id=device((z + d) % NZC, plane, core), device_id_type=MESH)

    for d in Z_STEPS:
        spread(d).start()
    loop(1, NZC, lambda d: spread(d).wait())
    total = zslots[0]
    for k in range(1, NZC):
        total += zslots[k]
    out[core, plane] = total

    def beyond(step):
        return (plane // 4 + step // 4) % 4 * 4 + (plane + step) % 4

    def gather(step):
        return pltpu.make_async_remote_copy(
            src_ref=out.at[core, plane], dst_ref=out.at[core, plane],
            send_sem=plane_sem.at[1, 0, step], recv_sem=plane_sem.at[1, 1, step],
            device_id=device(z, beyond(step), core), device_id_type=MESH)

    def forward(k):
        return core_copy(out.at[core, k], out.at[core, k], 4 + k)

    for step in PLANE_STEPS:
        gather(step).start()
    forward(plane).start()
    for step in PLANE_STEPS[::-1]:
        gather(step).wait_recv()
        forward(beyond((4 - step // 4) % 4 * 4 + (4 - step % 4) % 4)).start()
    loop(1, PLANE, lambda step: gather(step).wait_send())
    loop(0, PLANE, lambda k: forward(k).wait())


PAIRS = [(0, 0), (0, 1), (0, 2), (1, 1), (1, 2), (2, 2)]


def split(a):
    hi = a.astype(BF16)
    rest = a - hi.astype(F32)
    mid = rest.astype(BF16)
    return hi, mid, (rest - mid.astype(F32)).astype(BF16)


def dot(a, b, turned=False):
    dims = (((1,), (1 if turned else 0,)), ((), ()))
    n = a[0].shape[0]

    def term(count, j):
        left = a[0] if count == 1 else jnp.concatenate(a[:count], axis=0)
        out = lax.dot_general(left, b[j], dims, preferred_element_type=F32)
        return [out[n * i:n * i + n] for i in range(count)]

    hh, mh, lh = term(3, 0)
    hm, mm = term(2, 1)
    hl, = term(1, 2)
    return hh + (hm + mh + (hl + lh + mm))


def dot_wide(a, b):
    def wide(x, y, z, w):
        return jnp.dot(jnp.concatenate([x, y], axis=1), jnp.concatenate([z, w], axis=0), preferred_element_type=F32)

    return wide(a[0], a[1], b[0], b[0]) + (wide(a[0], a[1], b[1], b[1]) + wide(a[2], a[0], b[0], b[2]))


def gram_terms(high, mid, low):
    def term(a, b):
        return lax.dot_general(a, b, (((1,), (1,)), ((), ())), preferred_element_type=F32)

    return term(high, high) + term(mid, mid), term(high, mid) + term(high, low)


def store_gram(straight, crossed, part):
    for k, (a, b) in enumerate(PAIRS):
        rows, columns = slice(128 * a, 128 * a + 128), slice(128 * b, 128 * b + 128)
        block = straight[rows, columns] + (crossed[rows, columns] + crossed[columns, rows].T)
        flat = k * 128
        while flat < k * 128 + 128:
            inside = flat % 24
            size = min(24 - inside, k * 128 + 128 - flat)
            slab = flat // 24
            row = flat - k * 128
            part[slab // PLANE, slab % PLANE, inside:inside + size, :] = block[row:row + size]
            flat += size


def inverse_factor(cross, panel=16):
    rank = cross.shape[0]
    rows = lax.broadcasted_iota(jnp.int32, (panel, 128), 0)
    lanes = lax.broadcasted_iota(jnp.int32, (panel, 128), 1)
    here, rest = cross[:panel], cross[panel:]
    outs = []
    for first in range(0, rank, panel):
        end = first + panel
        columns = [jnp.broadcast_to(here[:, first + j:first + j + 1], (panel, 128)) for j in range(panel)]
        inside = (lanes >= first) & (lanes < end)
        solved = jnp.where(inside, (rows + first == lanes).astype(F32), here)
        lower = solved
        inverse = jnp.zeros((panel, 128), F32)
        value = jnp.broadcast_to(columns[0][:1], (8, 128))
        for k in range(panel):
            pivot = 1.0 / value
            if k + 1 < panel:
                one, two, three = (
                    jnp.broadcast_to(t, (8, 128))
                    for t in (columns[k + 1][k + 1:k + 2], columns[k][k + 1:k + 2], columns[k + 1][k:k + 1]))
                value = one - (two * three) * pivot
            pivot = jnp.concatenate([pivot] * (panel // 8), axis=0)
            ratio = columns[k] * pivot
            others = jnp.where(rows == k, 0.0, ratio)
            below = jnp.where(rows > k, ratio, 0.0)
            inverse = jnp.where(rows == k, pivot, inverse)
            for j in range(k + 1, panel):
                columns[j] = columns[j] - others * columns[j][k:k + 1]
            solved = solved - others * solved[k:k + 1]
            lower = lower - below * lower[k:k + 1]
        outs.append(jnp.where(lanes < end, lower * jnp.sqrt(inverse), 0.0))
        if end == rank:
            break
        solved = solved * inverse
        after = rest[:panel]
        here = jnp.where(inside, 0.0, after)
        for k in range(panel):
            here = here - jnp.broadcast_to(after[:, first + k:first + k + 1], (panel, 128)) * solved[k:k + 1]
        rest = rest[panel:]
        if end + panel == rank:
            continue

        def place(block):
            parts = [block, jnp.zeros((128 - end, 128), BF16)]
            if first:
                parts = [jnp.zeros((first, 128), BF16)] + parts
            return jnp.concatenate(parts, axis=0)

        high, mid, low = (place(t) for t in split(solved))
        a_high, a_mid, a_low = split(rest)

        def wide(a, b, c, d):
            return jnp.dot(
                jnp.concatenate([a, b], axis=1), jnp.concatenate([c, d], axis=0),
                preferred_element_type=F32)

        update = wide(a_high, a_mid, high, high) + (
            wide(a_high, a_mid, mid, mid) + wide(a_high, a_low, low, high))
        column = lax.broadcasted_iota(jnp.int32, update.shape, 1)
        rest = jnp.where((column >= first) & (column < end), 0.0, rest) - update
    return jnp.concatenate(outs, axis=0)


def iterate(packed, start, gram, own):
    blocks = packed[...].reshape(6, 128, 128)
    upper = {pair: blocks[k] for k, pair in enumerate(PAIRS)}
    full = jnp.concatenate([
        jnp.concatenate([upper[(a, b)] if a <= b else upper[(b, a)].T for b in range(3)], axis=1)
        for a in range(3)], axis=0)
    for k, term in enumerate(split(full)):
        gram[k] = term
    own[...] = start[...]

    def step(_):
        parts, cross = image_of(gram, own)
        own[...] = dot_wide(split(inverse_factor(cross)), parts)

    loop(0, ITERS - 1, step)


def image_of(gram, own):
    image = dot(split(own[...]), [gram[k] for k in range(3)])
    parts = split(jnp.concatenate([image, jnp.zeros((32, 384), F32)], axis=0))
    return parts, dot([t[:96] for t in parts], parts, turned=True)


def last_step(gram, own, others):
    parts, cross = image_of(gram, own)
    moved = [split(dot(parts, other)) for other in others]
    inverse = split(inverse_factor(cross))
    return [dot_wide(inverse, m) for m in moved], lambda: split(dot_wide(inverse, parts))


def own_rows(parts, first, count):
    row = lax.broadcasted_iota(jnp.int32, (count, 384), 0)
    pick = (lax.broadcasted_iota(jnp.int32, (count, 384), 1) == row + first).astype(BF16)
    dims = (((1,), (1,)), ((), ()))
    high, mid, low = (
        lax.dot_general(pick, t, dims, preferred_element_type=F32) for t in parts)
    return high + mid + low


def greet(barrier):
    gx, gy, z, plane, core = position()
    loop(1, GX, lambda d: signal(barrier, ((gx + d) % GX, gy)))
    signal(barrier, device(z, plane, 1 - core))
    loop(1, PLANE, lambda d: signal(barrier, device(z, (plane + d) % PLANE, core)))
    loop(1, NZC, lambda d: signal(barrier, device((z + d) % NZC, plane, core)))
    return GX - 1 + 1 + PLANE - 1 + NZC - 1


def window_kernel(cells_hbm, start_x_hbm, start_y_hbm, own_x, own_y, out, cells, start_x, start_y, send_x, field, field_terms,
                  send_y, planes, rows, send_c, basis, gram, sem_in, sem_x, sem_y, sem_c, *sums):
    gx, gy, _, _, _ = position()
    sums_x, sums_y = sums[:len(sums) // 2], sums[len(sums) // 2:]

    barrier = pltpu.get_barrier_semaphore()
    count = greet(barrier)

    def fetch(h):
        return pltpu.make_async_copy(cells_hbm.at[pl.ds(4 * h, 4)], cells.at[pl.ds(4 * h, 4)], sem_in.at[h])

    starts = [
        pltpu.make_async_copy(start_x_hbm, start_x, sem_in.at[CHUNKS]),
        pltpu.make_async_copy(start_y_hbm, start_y, sem_in.at[CHUNKS + 1])]
    for h in range(CHUNKS):
        fetch(h).start()
    for start in starts:
        start.start()

    def turn(h, to, target):
        for k in range(2):
            slabs = [
                cells[4 * h + 2 * k + i, pl.ds(pl.multiple_of(16 * (8 * z + to), 16), 16), :]
                for i in range(2) for z in range(4)]
            target[:, 128 * k:128 * k + 128] = jnp.concatenate(slabs, axis=0).T

    def copy_x(h, d):
        to = (gx // 4 + X_STEPS[d][0]) % 2 * 4 + (gx + X_STEPS[d][1]) % 4
        return pltpu.make_async_remote_copy(
            src_ref=send_x.at[h, to], dst_ref=field.at[h, gx],
            send_sem=sem_x.at[0, h, d], recv_sem=sem_x.at[1, h, d],
            device_id=(to, gy), device_id_type=MESH)

    for h in range(CHUNKS):
        fetch(h).wait()
        loop(1, GX, lambda d: turn(h, (gx + d) % GX, send_x.at[h, (gx + d) % GX]))
        if h == 0:
            pl.semaphore_wait(barrier, count)
        for d in range(GX - 1):
            copy_x(h, d).start()
    for h in range(CHUNKS):
        turn(h, gx, field.at[h, gx])
    straight, crossed = 0.0, 0.0
    for h in range(CHUNKS):
        for d in range(GX - 1):
            copy_x(h, d).wait_recv()
        terms = split(field[h].reshape(384, 256))
        for k in range(3):
            field_terms[h, k] = terms[k]
        more = gram_terms(*terms)
        straight, crossed = straight + more[0], crossed + more[1]
    store_gram(straight, crossed, sums_x[0])
    all_sum(*sums_x)
    for h in range(CHUNKS):
        for d in range(GX - 1):
            copy_x(h, d).wait_send()
    for start in starts:
        start.wait()
    iterate(sums_x[1], start_x, gram, basis)

    reduced_all, terms_x = last_step(
        gram, basis, [[field_terms[h, k] for k in range(3)] for h in range(CHUNKS)])
    for h, reduced in enumerate(reduced_all):
        for k in range(GY):
            send_y[k, :, 256 * h:256 * h + 256] = reduced[3 * k:3 * k + 3, :]

    def copy_y(d):
        step = Y_STEPS[d]
        to = (gy // 8 + step // 8) % 4 * 8 + (gy // 2 + step // 2) % 4 * 2 + (gy + step) % 2
        return pltpu.make_async_remote_copy(
            src_ref=send_y.at[to], dst_ref=planes.at[gy],
            send_sem=sem_y.at[0, d], recv_sem=sem_y.at[1, d],
            device_id=(gx, to), device_id_type=MESH)

    for d in range(GY - 1):
        copy_y(d).start()
    planes[gy] = send_y[gy]
    own_x[...] = own_rows(terms_x(), gx * 48, 48)
    for d in range(GY - 1):
        copy_y(d).wait()
    for y in range(12):
        pieces = [planes[:, r, 64 * y:64 * y + 64] for r in range(3)]
        pieces.append(jnp.zeros((GY, 64), F32))
        for k in range(2):
            rows[k, pl.ds(y, GY, stride=12), :] = jnp.concatenate(pieces[2 * k:2 * k + 2], axis=1)
    straight, crossed = gram_terms(*split(jnp.concatenate([rows[0], rows[1]], axis=1)))
    store_gram(straight, crossed, sums_y[0])
    all_sum(*sums_y)
    iterate(sums_y[1], start_y, gram, basis)

    (core,), terms_y = last_step(gram, basis, [split(jnp.concatenate([rows[0], rows[1]], axis=1))])
    for k in range(GY):
        send_c[k] = core[3 * k:3 * k + 3, :192]
    home = gy // 4
    slot = gx * 4 + gy % 4

    def copy_c(k, to):
        return pltpu.make_async_remote_copy(
            src_ref=send_c.at[k], dst_ref=out.at[to],
            send_sem=sem_c.at[0, k], recv_sem=sem_c.at[1, to],
            device_id=(home, k), device_id_type=MESH)

    def go(k):
        mine = (home == gx) & (k == gy)

        @pl.when(jnp.logical_not(mine))
        def _():
            copy_c(k, slot).start()

        @pl.when(mine)
        def _():
            out[slot] = send_c[k]

    def finish(k):
        @pl.when(jnp.logical_not((home == gx) & (k == gy)))
        def _():
            copy_c(k, slot).wait_send()

        @pl.when(jnp.logical_not((home == gx) & (k == slot)))
        def _():
            copy_c(k, k).wait_recv()

    loop(0, GY, lambda d: go((slot + d) % GY))
    own_y[...] = own_rows(terms_y(), gy * 12, 12)
    loop(0, GY, finish)


def results_kernel(own_x, own_y, pieces, basis_x, basis_y, core):
    basis_x[...] = own_x[...]
    basis_y[...] = own_y[...]
    for j in range(4):
        for s in range(3):
            block = jnp.concatenate([pieces[4 * i + j, s:s + 1, :] for i in range(8)], axis=0).T
            for r in range(3):
                quarters = [block[64 * r + 16 * z:64 * r + 16 * z + 16] for z in range(4)]
                core[3 * j + r, s] = jnp.concatenate(quarters, axis=1)


VM = pl.BlockSpec(memory_space=pltpu.VMEM)


def local(snapshot, start_x, start_y):
    cells = jnp.transpose(snapshot, (1, 2, 3, 0)).reshape(12, 512, 48)
    own_x, own_y, pieces = pl.pallas_call(
        window_kernel,
        out_shape=[jax.ShapeDtypeStruct(shape, F32) for shape in ((48, 96), (12, 96), (GY, 3, 192))],
        in_specs=[pl.BlockSpec(memory_space=pltpu.HBM)] * 3,
        out_specs=[VM] * 3,
        scratch_shapes=[
            pltpu.VMEM((12, 512, 48), F32),
            pltpu.VMEM((96, 384), F32),
            pltpu.VMEM((96, 384), F32),
            pltpu.VMEM((CHUNKS, GX, 48, 256), F32),
            pltpu.VMEM((CHUNKS, GX, 48, 256), F32),
            pltpu.VMEM((CHUNKS, 3, 384, 256), BF16),
            pltpu.VMEM((GY, 3, 768), F32),
            pltpu.VMEM((GY, 3, 768), F32),
            pltpu.VMEM((2, 384, 128), F32),
            pltpu.VMEM((GY, 3, 192), F32),
            pltpu.VMEM((96, 384), F32),
            pltpu.VMEM((3, 384, 384), BF16),
            pltpu.SemaphoreType.DMA((CHUNKS + 2,)),
            pltpu.SemaphoreType.DMA((2, CHUNKS, GX)),
            pltpu.SemaphoreType.DMA((2, GY)),
            pltpu.SemaphoreType.DMA((2, GY)),
        ] + sum_scratch() + sum_scratch(),
        compiler_params=pltpu.CompilerParams(
            collective_id=1, has_side_effects=True, vmem_limit_bytes=62 * 1024 * 1024),
        name="window",
    )(cells, start_x.T, start_y.T)
    basis_x, basis_y, core = pl.pallas_call(
        results_kernel,
        out_shape=[jax.ShapeDtypeStruct(shape, F32) for shape in ((48, 96), (12, 96), (12, 3, 16, 32))],
        in_specs=[VM] * 3,
        out_specs=[VM] * 3,
        compiler_params=pltpu.CompilerParams(vmem_limit_bytes=62 * 1024 * 1024),
        name="results",
    )(own_x, own_y, pieces)
    return (basis_x, basis_y, jnp.transpose(core, (0, 1, 3, 2)))


def solution(mesh):
    in_specs = (P("gx", "gy", None, None), P(), P())
    out_specs = (P("gx", None), P("gy", None), P("gx", "gy", None, None))
    return jax.shard_map(local, mesh=mesh, in_specs=in_specs, out_specs=out_specs, check_vma=False)
```
